256 devices in a mesh: ka: 64 (over z, x_lo, y), ba: 4 (over x_hi, core).
Axes of the slice: x: 4 (x_hi: 2, x_lo: 2; x = x_hi * 2 + x_lo), y: 4, z: 8, core: 2. Of those that a mesh axis runs over, the one named last changes fastest.
Arguments:
- orbitals: bfloat16 [64, 4, 2, 32, 1024], P('ka', 'ba'), may hold values from -6 to 6
- kpoints: int32 [64, 3], replicated, may hold values from 0 to 7, as said below
- occupied: int32 [64], replicated, may hold values from 1 to 4, as said below
Outputs:
- exchange_terms: float32 [64, 4, 2, 32, 1024], P('ka', 'ba')
The draws below stay inside these ranges and needn't reach their ends.
Inputs may be any that keep to these rules, and one draw needn't show every extreme that they name: `kpoints`: distinct points of the 8 x 8 x 8 k-mesh; the point (0, 0, 0) and the far corner are among them. Some k-point has all 4 bands occupied and some only one.
All inputs are finite; a program needn't handle non-finite values.
Results may differ from the reference program's by a relative error of at most 0.008.
Values may be sent and summed in bfloat16 or wider, within the bound.
No kernel may reach another device: no remote copies, remote signals or barrier semaphores. Data moves between devices by JAX's collectives and lax.ppermute only.
A program may use at most 64 MiB of HBM per device.

```python
import math
import jax
import jax.numpy as jnp
from jax import lax

GRID = 32
KMESH = 8
STEPS = 3
BANDS = 4
KPTS = 64


def draw_kpoints(key, part):
    key = jax.random.fold_in(key, 11)
    total_points = KMESH ** 3
    middle_order = jax.random.permutation(key, total_points - 2).astype(jnp.int32) + 1
    corner_pair = jnp.array([0, total_points - 1], dtype=jnp.int32)
    chosen = jnp.concatenate([corner_pair, middle_order[:KPTS - 2]])
    chosen = chosen[jax.random.permutation(jax.random.fold_in(key, 1), KPTS)]
    return jnp.stack([chosen // (KMESH * KMESH), chosen // KMESH % KMESH, chosen % KMESH], axis=1).astype(jnp.int32)


def draw_occupied(key, part):
    key = jax.random.fold_in(key, 23)
    counts_all = jax.random.randint(key, (KPTS,), 1, BANDS + 1, dtype=jnp.int32)
    return counts_all.at[0].set(BANDS).at[1].set(1)


def shard_levels(rng, extent, split, low, top_value):
    def one(axis_at, parts):
        steps = jax.random.uniform(jax.random.fold_in(jax.random.fold_in(rng, 6), axis_at), (parts,), jnp.float32, low / len(split), top_value / len(split))
        return jnp.repeat(jnp.exp(steps), extent[axis_at] // parts).reshape((-1,) + (1,) * (len(extent) - axis_at - 1))

    gain = one(*split[0])
    for cut in split[1:]:
        gain = gain * one(*cut)
    return gain


def centred(own_key, extent, spread, most, split=(), kind=jnp.bfloat16):
    result = jax.random.normal(own_key, extent, jnp.float32) * spread
    if len(split) > 0:
        result = shard_levels(own_key, extent, split, -0.22, 0.18) * result
    return jnp.clip(result, min=-most, max=most).astype(kind)


def setup_inputs(seed: int = 0) -> dict:
    arg_keys = jax.random.split(jax.random.key(seed), 4)
    orbitals = centred(arg_keys[0], (KPTS, BANDS, 2, GRID, GRID * GRID), 1.0, 6.0, ((0, 64), (1, 4)))
    kpoints = draw_kpoints(jax.random.fold_in(arg_keys[3], 71), 0)
    occupied = draw_occupied(jax.random.fold_in(arg_keys[3], 71), 0)
    return {"orbitals": orbitals, "kpoints": kpoints, "occupied": occupied}


cell_length = 20.52
screening = 0.05
prefactor = math.pi
pass_forms = ("aibj,pbjyz->paiyz", "aibj,pbxjz->paxiz", "aibj,pbxyj->paxyi")


def dft_table(grid_cells, sign_value):
    index_all = jnp.arange(grid_cells, dtype=jnp.int32)
    product_idx = (index_all[:, None] * index_all[None, :]) % grid_cells
    angle_all = (2.0 * math.pi / grid_cells) * product_idx.astype(jnp.float32)
    cosine = jnp.cos(angle_all)
    sine = sign_value * jnp.sin(angle_all)
    upper_half = jnp.concatenate([cosine, sine], axis=1)
    lower_half = jnp.concatenate([-sine, cosine], axis=1)
    return jnp.concatenate([upper_half, lower_half], axis=0).astype(jnp.bfloat16)


def kernel_table(grid_cells, mesh_points, own_point, other_point):
    half_mesh = mesh_points // 2
    offset_int = ((own_point - other_point + half_mesh) % mesh_points) - half_mesh
    shift_frac = offset_int.astype(jnp.float32) / mesh_points
    index_all = jnp.arange(grid_cells, dtype=jnp.int32)
    freq_int = (index_all + grid_cells // 2) % grid_cells - grid_cells // 2
    unit_step = 2.0 * math.pi / cell_length
    along_x = (freq_int.astype(jnp.float32) + shift_frac[0]) * unit_step
    along_y = (freq_int.astype(jnp.float32) + shift_frac[1]) * unit_step
    along_z = (freq_int.astype(jnp.float32) + shift_frac[2]) * unit_step
    squared = along_x[:, None, None] ** 2 + along_y[None, :, None] ** 2 + along_z[None, None, :] ** 2
    values_all = prefactor / (squared + screening) / float(grid_cells ** 3)
    return values_all.reshape(grid_cells, grid_cells * grid_cells)


def one_pass(field_in, table_in, axis_pos, out_type):
    pairs_count = field_in.shape[0]
    grid_cells = field_in.shape[2]
    rest_cells = field_in.shape[3]
    cube = field_in.reshape(pairs_count, 2, grid_cells, grid_cells, grid_cells).astype(jnp.float32)
    quad = table_in.astype(jnp.float32).reshape(2, grid_cells, 2, grid_cells)
    product_out = jnp.einsum(pass_forms[axis_pos], quad, cube,
                             precision=lax.Precision.HIGHEST).astype(out_type)
    return product_out.reshape(pairs_count, 2, grid_cells, rest_cells)


def pair_terms(own_bands, partner, kernel, own_occ, partner_occ, forward, inverse):
    def per_band(carry_in, scan_items):
        band_data, band_weight = scan_items
        band_re = band_data[0].astype(jnp.float32)
        band_im = band_data[1].astype(jnp.float32)
        mate_re = partner[:, 0].astype(jnp.float32)
        mate_im = partner[:, 1].astype(jnp.float32)
        density = jnp.stack([mate_re * band_re + mate_im * band_im,
                             mate_re * band_im - mate_im * band_re], axis=1).astype(jnp.bfloat16)
        first_out = one_pass(density, forward, 0, jnp.bfloat16)
        second_out = one_pass(first_out, forward, 1, jnp.bfloat16)
        third_out = one_pass(second_out, forward, 2, jnp.float32)
        scaled = (third_out * kernel).astype(jnp.bfloat16)
        back_one = one_pass(scaled, inverse, 0, jnp.bfloat16)
        back_two = one_pass(back_one, inverse, 1, jnp.bfloat16)
        wave = one_pass(back_two, inverse, 2, jnp.float32)
        wave_re = wave[:, 0]
        wave_im = wave[:, 1]
        mate_weight = partner_occ[:, None, None]
        k_real = -jnp.sum(mate_weight * (mate_re * wave_re - mate_im * wave_im), axis=0)
        k_imag = -jnp.sum(mate_weight * (mate_re * wave_im + mate_im * wave_re), axis=0)
        q_real = -band_weight * (band_re * wave_re + band_im * wave_im)
        q_imag = -band_weight * (band_im * wave_re - band_re * wave_im)
        return carry_in + jnp.stack([q_real, q_imag], axis=1), jnp.stack([k_real, k_imag], axis=0)

    start_sum = jnp.zeros((partner.shape[0], 2) + partner.shape[2:], jnp.float32)
    q_term, k_term = lax.scan(per_band, start_sum, (own_bands, own_occ))
    return k_term, q_term


def reference(orbitals, kpoints, occupied):
    forward = dft_table(GRID, 1.0)
    inverse = dft_table(GRID, -1.0)
    occupancy = (jnp.arange(BANDS, dtype=jnp.int32)[None, :] < occupied[:, None]).astype(jnp.float32)
    exchange_sum = jnp.zeros(orbitals.shape, jnp.float32)
    for step_index in range(1, STEPS + 1):
        partners = jnp.roll(orbitals, step_index, axis=0)
        partner_points = jnp.roll(kpoints, step_index, axis=0)
        partner_occ = jnp.roll(occupancy, step_index, axis=0)

        def per_point(point_items):
            own_bands, mate_bands, own_point, mate_point, own_weight, mate_weight = point_items
            kernel = kernel_table(GRID, KMESH, own_point, mate_point)
            return pair_terms(own_bands, mate_bands, kernel, own_weight, mate_weight, forward, inverse)

        k_terms, q_terms = lax.map(per_point, (orbitals, partners, kpoints, partner_points, occupancy, partner_occ))
        exchange_sum = exchange_sum + k_terms + jnp.roll(q_terms, -step_index, axis=0)
    return exchange_sum
```

```python
import functools
import math

import jax
import jax.numpy as jnp
import numpy as np
from jax import lax
from jax.experimental import pallas as pl
from jax.experimental.pallas import tpu as pltpu
from jax.sharding import PartitionSpec as P

KMESH = 8
STEPS = 3
GRID = 32
LANES = 128
CELL = 20.52
SCREENING = 0.05


def complex_table(angle):
    cosine, sine = np.cos(angle), np.sin(angle)
    return np.block([[cosine, sine], [-sine, cosine]])


def first_tables():
    a, x = [v.reshape(-1) for v in np.meshgrid(np.arange(4), np.arange(32), indexing="ij")]
    tables = []
    for b in range(2):
        turns = x[:, None] * x[None, :] + 8 * a[:, None] * a[None, :] + 4 * b * a[:, None]
        tables.append(complex_table(2 * math.pi / 32 * (turns % 32)))
    return np.stack(tables).astype(jnp.bfloat16)


def second_tables():
    low, z = [v.reshape(-1) for v in np.meshgrid(np.arange(4), np.arange(32), indexing="ij")]
    tables = []
    for k1 in range(8):
        turns = low[:, None] * (k1 + 8 * low[None, :]) + z[:, None] * z[None, :]
        tables.append(complex_table(2 * math.pi / 32 * (turns % 32).T).T)
    return np.stack(tables).astype(jnp.bfloat16)


def block(index):
    return slice(index * LANES, (index + 1) * LANES)


def rows(index):
    return slice(index * GRID, (index + 1) * GRID)


def dot(left, right, dims=((1,), (0,))):
    return lax.dot_general(left, right, (dims, ((), ())), preferred_element_type=jnp.float32)


def pair_kernel(step, n_count, first, kpoints, occupied, spot, mate, *refs):
    bands = refs[:n_count]
    refs = refs[n_count:]
    sums_in = None if first else refs[0]
    refs = refs if first else refs[1:]
    forward_x, inverse_x, forward_yz, inverse_yz, mate_out, sums, wide, mid, back = refs

    count = kpoints.shape[0]
    own = spot[0]
    slot = spot[1]
    other = lax.rem(own - step + count, count)
    along = []
    for i in range(3):
        apart = lax.rem(kpoints[own, i] - kpoints[other, i] + KMESH // 2 + KMESH, KMESH)
        along.append((apart - KMESH // 2).astype(jnp.float32) / KMESH)
    mate_weight = jnp.where(slot < occupied[other], -1.0, 0.0)
    unit = 2 * math.pi / CELL

    def centred(index):
        return jnp.bitwise_and(index + GRID // 2, GRID - 1) - GRID // 2

    shape = (GRID, LANES)
    lane = lax.broadcasted_iota(jnp.int32, shape, 1)
    at_x = (centred(lax.broadcasted_iota(jnp.int32, shape, 0)).astype(jnp.float32) + along[0]) * unit
    at_z = (centred(jnp.bitwise_and(lane, GRID - 1)).astype(jnp.float32) + along[2]) * unit
    high = lax.shift_right_logical(lane, 5) * 8

    for b in range(2):
        for a in range(4):
            cut = block(2 * a + b)
            mate_re = mate[0, :, cut].astype(jnp.float32)
            mate_im = mate[1, :, cut].astype(jnp.float32)
            for n in range(n_count):
                band_re = bands[n][0, :, cut].astype(jnp.float32)
                band_im = bands[n][1, :, cut].astype(jnp.float32)
                wide[b, rows(a), block(n)] = (mate_re * band_re + mate_im * band_im).astype(jnp.bfloat16)
                wide[b, rows(4 + a), block(n)] = (mate_re * band_im - mate_im * band_re).astype(jnp.bfloat16)

    for n in range(0, n_count, 2):
        pair = slice(n * LANES, (n + 2) * LANES)
        even = dot(forward_x[0], wide[0, :, pair])
        odd = dot(forward_x[1], wide[1, :, pair])
        plus = (even + odd).astype(jnp.bfloat16)
        minus = (even - odd).astype(jnp.bfloat16)
        for i in range(2):
            for e in range(4):
                for c in range(2):
                    mid[e, rows(n + i), block(c)] = plus[rows(4 * c + e), block(i)]
                    mid[e + 4, rows(n + i), block(c)] = minus[rows(4 * c + e), block(i)]

    for e in range(4):
        halves = []
        for k1 in (e, e + 4):
            third = dot(mid[k1], forward_yz[k1])
            at_y = (centred(high + k1).astype(jnp.float32) + along[1]) * unit
            squared = at_x * at_x + at_y * at_y + at_z * at_z
            screened = (math.pi / GRID**3) / (squared + SCREENING)
            screened = jnp.concatenate([screened, screened], axis=1)
            screened = jnp.concatenate([screened] * n_count, axis=0)
            halves.append(dot((third * screened).astype(jnp.bfloat16), inverse_yz[k1]))
        for b in range(2):
            joined = (halves[0] + halves[1] if b == 0 else halves[0] - halves[1]).astype(jnp.bfloat16)
            for n in range(n_count):
                for c in range(2):
                    back[b, rows(4 * c + e), block(n)] = joined[rows(n), block(c)]

    for b in range(2):
        for n in range(0, n_count, 2):
            pair = slice(n * LANES, (n + 2) * LANES)
            wide_out = dot(inverse_x[b], back[b, :, pair])
            for a in range(4):
                cut = block(2 * a + b)
                mate_re = mate[0, :, cut].astype(jnp.float32) * mate_weight
                mate_im = mate[1, :, cut].astype(jnp.float32) * mate_weight
                total_re = total_im = None
                for i in range(2):
                    band = slot ^ (n + i)
                    weight = jnp.where(band < occupied[own], -1.0, 0.0)
                    wave_re = wide_out[rows(a), block(i)]
                    wave_im = wide_out[rows(4 + a), block(i)]
                    term_re = mate_re * wave_re - mate_im * wave_im
                    term_im = mate_re * wave_im + mate_im * wave_re
                    if not first:
                        term_re = term_re + sums_in[n + i, 0, :, cut]
                        term_im = term_im + sums_in[n + i, 1, :, cut]
                    sums[n + i, 0, :, cut] = term_re
                    sums[n + i, 1, :, cut] = term_im
                    band_re = bands[n + i][0, :, cut].astype(jnp.float32) * weight
                    band_im = bands[n + i][1, :, cut].astype(jnp.float32) * weight
                    back_re = band_re * wave_re + band_im * wave_im
                    back_im = band_im * wave_re - band_re * wave_im
                    total_re = back_re if total_re is None else total_re + back_re
                    total_im = back_im if total_im is None else total_im + back_im
                if n == 0:
                    mate_out[0, :, cut] = total_re
                    mate_out[1, :, cut] = total_im
                else:
                    mate_out[0, :, cut] += total_re
                    mate_out[1, :, cut] += total_im


def pair_terms(step, kpoints, occupied, spot, mate, bands, sums, tables):
    n_count = len(bands)
    smem = pl.BlockSpec(memory_space=pltpu.SMEM)
    vmem = pl.BlockSpec(memory_space=pltpu.VMEM)
    first = sums is None
    field = mate.shape
    operands = [mate, *bands] + ([] if first else [sums]) + list(tables)
    return pl.pallas_call(
        functools.partial(pair_kernel, step, n_count, first),
        out_shape=[
            jax.ShapeDtypeStruct(field, jnp.float32),
            jax.ShapeDtypeStruct((n_count,) + field, jnp.float32),
        ],
        in_specs=[smem] * 3 + [vmem] * len(operands),
        out_specs=[vmem, vmem],
        scratch_shapes=[
            pltpu.VMEM((2, 256, n_count * LANES), jnp.bfloat16),
            pltpu.VMEM((8, n_count * GRID, 256), jnp.bfloat16),
            pltpu.VMEM((2, 256, n_count * LANES), jnp.bfloat16),
        ],
        compiler_params=pltpu.CompilerParams(vmem_limit_bytes=32 * 1024 * 1024),
        cost_estimate=pl.CostEstimate(flops=2 * 10**9, bytes_accessed=6 * 10**6, transcendentals=0),
    )(kpoints, occupied, spot, *operands)


def passed_along(value, by):
    count = lax.axis_size("ka")
    return lax.ppermute(value, "ka", [(i, (i + by) % count) for i in range(count)])


def swapped(value, flip):
    return lax.ppermute(value, "ba", [(i, i ^ flip) for i in range(lax.axis_size("ba"))])


def on_device(orbitals, kpoints, occupied):
    own = orbitals[0, 0]
    spot = jnp.stack([lax.axis_index("ka"), lax.axis_index("ba")])
    forward_x = first_tables()
    forward_yz = second_tables()
    tables = (
        jnp.asarray(forward_x),
        jnp.asarray(forward_x.transpose(0, 2, 1)),
        jnp.asarray(forward_yz),
        jnp.asarray(forward_yz.transpose(0, 2, 1)),
    )
    mates = [passed_along(own, step) for step in range(1, STEPS + 1)]
    bands = [own] + [swapped(own, flip) for flip in (1, 2, 3)]
    sums = None
    total = None
    for step in range(1, STEPS + 1):
        mate_term, sums = pair_terms(
            step, kpoints, occupied, spot, mates[step - 1], bands, sums, tables
        )
        returned = passed_along(mate_term.astype(jnp.bfloat16), -step).astype(jnp.float32)
        total = returned if total is None else total + returned
    total = total + sums[0]
    for flip in (1, 2, 3):
        total = total + swapped(sums[flip].astype(jnp.bfloat16), flip).astype(jnp.float32)
    return total[None, None]


def solution(mesh):
    in_specs = (P("ka", "ba", None, None, None), P(), P())
    out_specs = P("ka", "ba", None, None, None)
    return jax.shard_map(
        on_device, mesh=mesh, in_specs=in_specs, out_specs=out_specs, check_vma=False
    )
```

```python
import functools
import math

import jax
import jax.numpy as jnp
import numpy as np
from jax import lax
from jax.experimental import pallas as pl
from jax.experimental.pallas import tpu as pltpu
from jax.sharding import PartitionSpec as P

KMESH = 8
SHIFTS = (1, 3, -2)
GRID = 32
LANES = 128
CELL = 20.52
SCREENING = 0.05
VMEM_BYTES = 32 * 1024 * 1024


def complex_table(angle):
    cosine, sine = np.cos(angle), np.sin(angle)
    return np.block([[cosine, sine], [-sine, cosine]])


def first_tables():
    a, x = [v.reshape(-1) for v in np.meshgrid(np.arange(4), np.arange(32), indexing="ij")]
    tables = []
    for b in range(2):
        turns = x[:, None] * x[None, :] + 8 * a[:, None] * a[None, :] + 4 * b * a[:, None]
        tables.append(complex_table(2 * math.pi / 32 * (turns % 32)))
    return np.stack(tables).astype(jnp.bfloat16)


def second_tables():
    low, z = [v.reshape(-1) for v in np.meshgrid(np.arange(4), np.arange(32), indexing="ij")]
    tables = []
    for k1 in range(8):
        turns = low[:, None] * (k1 + 8 * low[None, :]) + z[:, None] * z[None, :]
        tables.append(complex_table(2 * math.pi / 32 * (turns % 32).T).T)
    return np.stack(tables).astype(jnp.bfloat16)


def block(index):
    return slice(index * LANES, (index + 1) * LANES)


def rows(index):
    return slice(index * GRID, (index + 1) * GRID)


def dot(left, right, dims=((1,), (0,))):
    return lax.dot_general(left, right, (dims, ((), ())), preferred_element_type=jnp.float32)


def stage_kernel(kpoints, spot, *refs):
    tables = refs[:4]
    staged = refs[4:8]
    screened, sems = refs[8:]
    copies = [pltpu.make_async_copy(tables[i], staged[i], sems.at[i]) for i in range(4)]
    for copy in copies:
        copy.start()

    count = kpoints.shape[1]
    own = spot[0]
    unit = 2 * math.pi / CELL
    shape = (GRID, LANES)
    lane = lax.broadcasted_iota(jnp.int32, shape, 1)
    high = lax.shift_right_logical(lane, 5) * 8

    def centred(index):
        return (jnp.bitwise_and(index + GRID // 2, GRID - 1) - GRID // 2).astype(jnp.float32)

    grid_x = centred(lax.broadcasted_iota(jnp.int32, shape, 0))
    grid_z = centred(jnp.bitwise_and(lane, GRID - 1))
    for at, step in enumerate(SHIFTS):
        other = lax.rem(own - step + count, count)
        later, earlier = (own, other) if step > 0 else (other, own)
        along = []
        for i in range(3):
            apart = lax.rem(kpoints[i, later] - kpoints[i, earlier] + KMESH // 2 + KMESH, KMESH)
            along.append((apart - KMESH // 2).astype(jnp.float32) / KMESH)
        at_x = (grid_x + along[0]) * unit
        at_z = (grid_z + along[2]) * unit
        flat = at_x * at_x + at_z * at_z + SCREENING
        for k1 in range(8):
            at_y = (centred(high + k1) + along[1]) * unit
            screened[at, k1] = (math.pi / GRID**3) / (flat + at_y * at_y)
    for copy in copies:
        copy.wait()


def staged(kpoints, spot, tables):
    smem = pl.BlockSpec(memory_space=pltpu.SMEM)
    vmem = pl.BlockSpec(memory_space=pltpu.VMEM)
    return pl.pallas_call(
        stage_kernel,
        out_shape=[jax.ShapeDtypeStruct(t.shape, t.dtype) for t in tables]
        + [jax.ShapeDtypeStruct((len(SHIFTS), 8, GRID, LANES), jnp.float32)],
        in_specs=[smem] * 2 + [pl.BlockSpec(memory_space=pl.ANY)] * 4,
        out_specs=[vmem] * 5,
        scratch_shapes=[pltpu.SemaphoreType.DMA((4,))],
        compiler_params=pltpu.CompilerParams(vmem_limit_bytes=VMEM_BYTES),
        cost_estimate=pl.CostEstimate(flops=10**6, bytes_accessed=6 * 10**6, transcendentals=0),
    )(kpoints, spot, *tables)


def pair_kernel(at, flips, has_sums, has_mate, occupied, spot, mate, *refs):
    groups = len(flips)
    refs = list(refs)

    def take(n):
        taken = refs[:n]
        del refs[:n]
        return taken

    bands = take(groups)
    sums_in = take(groups) if has_sums else None
    mate_in = take(1)[0] if has_mate else None
    forward_x, inverse_x, forward_yz, inverse_yz, screened, mate_out = take(6)
    sums = take(groups)
    wide, mid, back = refs

    step = SHIFTS[at]
    turned = step < 0
    count = occupied.shape[0]
    own = spot[0]
    slot = spot[1]
    other = lax.rem(own - step + count, count)
    mate_weight = jnp.where(slot < occupied[other], -1.0, 0.0)

    for b in range(2):
        for a in range(4):
            cut = block(2 * a + b)
            mate_re = mate[0, :, cut].astype(jnp.float32)
            mate_im = mate[1, :, cut].astype(jnp.float32)
            for g in range(groups):
                for i in range(2):
                    band_re = bands[g][i, 0, :, cut].astype(jnp.float32)
                    band_im = bands[g][i, 1, :, cut].astype(jnp.float32)
                    value_re = mate_re * band_re + mate_im * band_im
                    if turned:
                        value_im = mate_im * band_re - mate_re * band_im
                    else:
                        value_im = mate_re * band_im - mate_im * band_re
                    wide[b, g, rows(a), block(i)] = value_re.astype(jnp.bfloat16)
                    wide[b, g, rows(4 + a), block(i)] = value_im.astype(jnp.bfloat16)

    for g in range(groups):
        even = dot(forward_x[0], wide[0, g])
        odd = dot(forward_x[1], wide[1, g])
        plus = (even + odd).astype(jnp.bfloat16)
        minus = (even - odd).astype(jnp.bfloat16)
        for i in range(2):
            for e in range(4):
                for c in range(2):
                    mid[e, rows(2 * g + i), block(c)] = plus[rows(4 * c + e), block(i)]
                    mid[e + 4, rows(2 * g + i), block(c)] = minus[rows(4 * c + e), block(i)]

    for e in range(4):
        halves = []
        for k1 in (e, e + 4):
            third = dot(mid[k1], forward_yz[k1])
            factor = screened[at, k1]
            factor = jnp.concatenate([factor, factor], axis=1)
            factor = jnp.concatenate([factor] * (2 * groups), axis=0)
            halves.append(dot((third * factor).astype(jnp.bfloat16), inverse_yz[k1]))
        for b in range(2):
            joined = (halves[0] - halves[1] if b else halves[0] + halves[1]).astype(jnp.bfloat16)
            for g in range(groups):
                for i in range(2):
                    for c in range(2):
                        back[b, g, rows(4 * c + e), block(i)] = joined[rows(2 * g + i), block(c)]

    for b in range(2):
        waves = [dot(inverse_x[b], back[b, g]) for g in range(groups)]
        for a in range(4):
            cut = block(2 * a + b)
            mate_re = mate[0, :, cut].astype(jnp.float32) * mate_weight
            mate_im = mate[1, :, cut].astype(jnp.float32) * mate_weight
            total_re = mate_in[0, :, cut] if has_mate else 0.0
            total_im = mate_in[1, :, cut] if has_mate else 0.0
            for g in range(groups):
                for i in range(2):
                    weight = jnp.where((slot ^ flips[g][i]) < occupied[own], -1.0, 0.0)
                    wave_re = waves[g][rows(a), block(i)]
                    wave_im = waves[g][rows(4 + a), block(i)]
                    band_re = bands[g][i, 0, :, cut].astype(jnp.float32) * weight
                    band_im = bands[g][i, 1, :, cut].astype(jnp.float32) * weight
                    if turned:
                        term_re = mate_re * wave_re + mate_im * wave_im
                        term_im = mate_im * wave_re - mate_re * wave_im
                        total_re = total_re + (band_re * wave_re - band_im * wave_im)
                        total_im = total_im + (band_re * wave_im + band_im * wave_re)
                    else:
                        term_re = mate_re * wave_re - mate_im * wave_im
                        term_im = mate_re * wave_im + mate_im * wave_re
                        total_re = total_re + (band_re * wave_re + band_im * wave_im)
                        total_im = total_im + (band_im * wave_re - band_re * wave_im)
                    if has_sums:
                        term_re = term_re + sums_in[g][i, 0, :, cut]
                        term_im = term_im + sums_in[g][i, 1, :, cut]
                    sums[g][i, 0, :, cut] = term_re.astype(sums[g].dtype)
                    sums[g][i, 1, :, cut] = term_im.astype(sums[g].dtype)
            mate_out[0, :, cut] = total_re.astype(mate_out.dtype)
            mate_out[1, :, cut] = total_im.astype(mate_out.dtype)


def pair_terms(at, flips, occupied, spot, mate, bands, tables, sums=(), mate_sum=(), types=None):
    groups = len(bands)
    mate_type, sums_type = types or (jnp.bfloat16, jnp.float32)
    smem = pl.BlockSpec(memory_space=pltpu.SMEM)
    vmem = pl.BlockSpec(memory_space=pltpu.VMEM)
    operands = [mate, *bands, *sums, *mate_sum, *tables]
    return pl.pallas_call(
        functools.partial(pair_kernel, at, flips, len(sums) > 0, len(mate_sum) > 0),
        out_shape=[jax.ShapeDtypeStruct(mate.shape, mate_type)]
        + [jax.ShapeDtypeStruct(band.shape, sums_type) for band in bands],
        in_specs=[smem] * 2 + [vmem] * len(operands),
        out_specs=[vmem] * (1 + groups),
        scratch_shapes=[
            pltpu.VMEM((2, groups, 256, 256), jnp.bfloat16),
            pltpu.VMEM((8, groups * 2 * GRID, 256), jnp.bfloat16),
            pltpu.VMEM((2, groups, 256, 256), jnp.bfloat16),
        ],
        compiler_params=pltpu.CompilerParams(vmem_limit_bytes=VMEM_BYTES),
        cost_estimate=pl.CostEstimate(
            flops=groups * 10**9, bytes_accessed=groups * 10**6, transcendentals=0
        ),
    )(occupied, spot, *operands)


def passed_along(value, by):
    count = lax.axis_size("ka")
    return lax.ppermute(value, "ka", [(i, (i + by) % count) for i in range(count)])


def swapped(value, flip):
    return lax.ppermute(value, "ba", [(i, i ^ flip) for i in range(lax.axis_size("ba"))])


def on_device(orbitals, kpoints, occupied):
    own = orbitals[0, 0]
    spot = jnp.stack([lax.axis_index("ka"), lax.axis_index("ba")])
    forward_x = first_tables()
    forward_yz = second_tables()
    tables = staged(
        kpoints.T,
        spot,
        (forward_x, forward_x.transpose(0, 2, 1), forward_yz, forward_yz.transpose(0, 2, 1)),
    )
    near = jnp.stack([own, swapped(own, 2)])
    mates = [passed_along(own, step) for step in SHIFTS]
    far = swapped(near, 1)
    near_flips, far_flips = (0, 2), (1, 3)
    both = (near_flips, far_flips)

    term, *sums = pair_terms(0, both, occupied, spot, mates[0], (near, far), tables)
    back = [passed_along(term, -SHIFTS[0])]
    term, *sums = pair_terms(1, both, occupied, spot, mates[1], (near, far), tables, sums=sums)
    back.append(passed_along(term, -SHIFTS[1]))
    part, far_sum = pair_terms(
        2, (far_flips,), occupied, spot, mates[2], (far,), tables,
        sums=sums[1:], types=(jnp.float32, jnp.bfloat16),
    )
    from_core = swapped(far_sum, 1)
    term, near_sum = pair_terms(
        2, (near_flips,), occupied, spot, mates[2], (near,), tables, sums=sums[:1], mate_sum=(part,)
    )
    across = swapped((near_sum[1] + from_core[1].astype(jnp.float32)).astype(jnp.bfloat16), 2)
    back.append(passed_along(term, -SHIFTS[2]))
    total = near_sum[0] + from_core[0].astype(jnp.float32) + across.astype(jnp.float32)
    for returned in back:
        total = total + returned.astype(jnp.float32)
    return total[None, None]


def solution(mesh):
    in_specs = (P("ka", "ba", None, None, None), P(), P())
    out_specs = P("ka", "ba", None, None, None)
    return jax.shard_map(
        on_device, mesh=mesh, in_specs=in_specs, out_specs=out_specs, check_vma=False
    )
```

```python
import functools
import math

import jax
import jax.numpy as jnp
from jax import lax
from jax.experimental import pallas as pl
from jax.experimental.pallas import tpu as pltpu
from jax.sharding import PartitionSpec as P

KMESH = 8
SHIFTS = (1, 3, -2)
GRID = 32
LANES = 128
CELL = 20.52
SCREENING = 0.05
VMEM_BYTES = 32 * 1024 * 1024


def block(index):
    return slice(index * LANES, (index + 1) * LANES)


def rows(index):
    return slice(index * GRID, (index + 1) * GRID)


def dot(left, right, dims=((1,), (0,))):
    return lax.dot_general(left, right, (dims, ((), ())), preferred_element_type=jnp.float32)


def stage_kernel(kpoints, occupied, spot, forward_x, inverse_x, forward_yz, inverse_yz, screened, weights):
    turn = 2 * math.pi / GRID
    square = (LANES, LANES)
    row = lax.broadcasted_iota(jnp.int32, square, 0)
    column = lax.broadcasted_iota(jnp.int32, square, 1)
    row_high, column_high = lax.shift_right_logical(row, 5), lax.shift_right_logical(column, 5)

    def wave(turns):
        turns = (jnp.bitwise_and(turns + GRID // 2, GRID - 1) - GRID // 2).astype(jnp.float32) * turn
        return jnp.cos(turns), jnp.sin(turns)

    def put(table, at, upper, lower):
        table[at, :LANES] = jnp.concatenate(upper, axis=1).astype(table.dtype)
        table[at, LANES:] = jnp.concatenate(lower, axis=1).astype(table.dtype)

    low = jnp.bitwise_and(row, GRID - 1) * jnp.bitwise_and(column, GRID - 1)
    cosine, sine = wave(8 * row_high * column_high + low)
    row_cosine, row_sine = wave(row_high)
    column_cosine, column_sine = wave(column_high)
    down = across = (cosine, sine)
    for k1 in range(8):
        put(forward_yz, k1, (down[0], -down[1]), (down[1], down[0]))
        put(inverse_yz, k1, (across[0], across[1]), (-across[1], across[0]))
        if k1 % 4 == 0:
            put(forward_x, k1 // 4, (down[0], down[1]), (-down[1], down[0]))
            put(inverse_x, k1 // 4, (across[0], -across[1]), (across[1], across[0]))
        down = (
            down[0] * row_cosine - down[1] * row_sine,
            down[0] * row_sine + down[1] * row_cosine,
        )
        across = (
            across[0] * column_cosine - across[1] * column_sine,
            across[0] * column_sine + across[1] * column_cosine,
        )

    count = kpoints.shape[1]
    own = spot[0]
    slot = spot[1]
    unit = 2 * math.pi / CELL
    shape = (GRID, LANES)
    lane = lax.broadcasted_iota(jnp.int32, shape, 1)
    high = lax.shift_right_logical(lane, 5) * 8

    def centred(index):
        return (jnp.bitwise_and(index + GRID // 2, GRID - 1) - GRID // 2).astype(jnp.float32)

    def occupancy(point, band):
        return jnp.full((1, LANES), jnp.where(band < occupied[point], -1.0, 0.0), jnp.float32)

    grid_x = centred(lax.broadcasted_iota(jnp.int32, shape, 0))
    grid_z = centred(jnp.bitwise_and(lane, GRID - 1))
    for at, step in enumerate(SHIFTS):
        other = lax.rem(own - step + count, count)
        later, earlier = (own, other) if step > 0 else (other, own)
        along = []
        for i in range(3):
            apart = lax.rem(kpoints[i, later] - kpoints[i, earlier] + KMESH // 2 + KMESH, KMESH)
            along.append((apart - KMESH // 2).astype(jnp.float32) / KMESH)
        at_x = (grid_x + along[0]) * unit
        at_z = (grid_z + along[2]) * unit
        flat = at_x * at_x + at_z * at_z + SCREENING
        for k1 in range(8):
            at_y = (centred(high + k1) + along[1]) * unit
            screened[at, k1] = (math.pi / GRID**3) / (flat + at_y * at_y)
        weights[4 + at] = occupancy(other, slot)
    for flip in range(4):
        weights[flip] = occupancy(own, slot ^ flip)


def staged(kpoints, occupied, spot):
    smem = pl.BlockSpec(memory_space=pltpu.SMEM)
    vmem = pl.BlockSpec(memory_space=pltpu.VMEM)
    return pl.pallas_call(
        stage_kernel,
        out_shape=[
            jax.ShapeDtypeStruct((2, 256, 256), jnp.bfloat16),
            jax.ShapeDtypeStruct((2, 256, 256), jnp.bfloat16),
            jax.ShapeDtypeStruct((8, 256, 256), jnp.bfloat16),
            jax.ShapeDtypeStruct((8, 256, 256), jnp.bfloat16),
            jax.ShapeDtypeStruct((len(SHIFTS), 8, GRID, LANES), jnp.float32),
            jax.ShapeDtypeStruct((4 + len(SHIFTS), 1, LANES), jnp.float32),
        ],
        in_specs=[smem] * 3,
        out_specs=[vmem] * 6,
        compiler_params=pltpu.CompilerParams(vmem_limit_bytes=VMEM_BYTES),
        cost_estimate=pl.CostEstimate(flops=10**6, bytes_accessed=6 * 10**6, transcendentals=0),
    )(kpoints, occupied, spot)


def pair_kernel(ats, flips, has_sums, has_mates, *refs):
    groups = len(flips)
    refs = list(refs)

    def take(n):
        taken = refs[:n]
        del refs[:n]
        return taken

    mates = take(len(ats))
    bands = [take(2) for _ in range(groups)]
    sums_in = take(groups) if has_sums else None
    mates_in = take(len(ats)) if has_mates else None
    forward_x, inverse_x, forward_yz, inverse_yz, screened, weights = take(6)
    mates_out = take(len(ats))
    sums = take(groups)
    wide, mid, back = refs
    jobs = [(m, g) for m in range(len(ats)) for g in range(groups)]

    for b in range(2):
        for a in range(4):
            cut = block(2 * a + b)
            for job, (m, g) in enumerate(jobs):
                mate_re = mates[m][0, :, cut].astype(jnp.float32)
                mate_im = mates[m][1, :, cut].astype(jnp.float32)
                for i in range(2):
                    band_re = bands[g][i][0, :, cut].astype(jnp.float32)
                    band_im = bands[g][i][1, :, cut].astype(jnp.float32)
                    value_re = mate_re * band_re + mate_im * band_im
                    if SHIFTS[ats[m]] < 0:
                        value_im = mate_im * band_re - mate_re * band_im
                    else:
                        value_im = mate_re * band_im - mate_im * band_re
                    wide[b, job, rows(a), block(i)] = value_re.astype(jnp.bfloat16)
                    wide[b, job, rows(4 + a), block(i)] = value_im.astype(jnp.bfloat16)

    for job in range(len(jobs)):
        even = dot(forward_x[0], wide[0, job])
        odd = dot(forward_x[1], wide[1, job])
        plus = (even + odd).astype(jnp.bfloat16)
        minus = (even - odd).astype(jnp.bfloat16)
        for i in range(2):
            for e in range(4):
                for c in range(2):
                    mid[e, rows(2 * job + i), block(c)] = plus[rows(4 * c + e), block(i)]
                    mid[e + 4, rows(2 * job + i), block(c)] = minus[rows(4 * c + e), block(i)]

    for e in range(4):
        halves = []
        for k1 in (e, e + 4):
            third = dot(mid[k1], forward_yz[k1])
            factor = []
            for at in ats:
                factor += [jnp.concatenate([screened[at, k1]] * 2, axis=1)] * (2 * groups)
            factor = jnp.concatenate(factor, axis=0)
            halves.append(dot((third * factor).astype(jnp.bfloat16), inverse_yz[k1]))
        for b in range(2):
            joined = (halves[0] - halves[1] if b else halves[0] + halves[1]).astype(jnp.bfloat16)
            for job in range(len(jobs)):
                for i in range(2):
                    for c in range(2):
                        back[b, job, rows(4 * c + e), block(i)] = joined[rows(2 * job + i), block(c)]

    for b in range(2):
        waves = [dot(inverse_x[b], back[b, job]) for job in range(len(jobs))]
        for a in range(4):
            cut = block(2 * a + b)
            mate_total = [[m[0, :, cut], m[1, :, cut]] if has_mates else [0.0, 0.0] for m in mates_in or ats]
            band_total = [[[s[i, 0, :, cut], s[i, 1, :, cut]] if has_sums else [0.0, 0.0] for i in range(2)] for s in sums_in or flips]
            for job, (m, g) in enumerate(jobs):
                mate_weight = weights[4 + ats[m]]
                mate_re = mates[m][0, :, cut].astype(jnp.float32) * mate_weight
                mate_im = mates[m][1, :, cut].astype(jnp.float32) * mate_weight
                for i in range(2):
                    weight = weights[flips[g][i]]
                    wave_re = waves[job][rows(a), block(i)]
                    wave_im = waves[job][rows(4 + a), block(i)]
                    band_re = bands[g][i][0, :, cut].astype(jnp.float32) * weight
                    band_im = bands[g][i][1, :, cut].astype(jnp.float32) * weight
                    to_mate, to_band = mate_total[m], band_total[g][i]
                    if SHIFTS[ats[m]] < 0:
                        to_band[0] += mate_re * wave_re + mate_im * wave_im
                        to_band[1] += mate_im * wave_re - mate_re * wave_im
                        to_mate[0] += band_re * wave_re - band_im * wave_im
                        to_mate[1] += band_re * wave_im + band_im * wave_re
                    else:
                        to_band[0] += mate_re * wave_re - mate_im * wave_im
                        to_band[1] += mate_re * wave_im + mate_im * wave_re
                        to_mate[0] += band_re * wave_re + band_im * wave_im
                        to_mate[1] += band_im * wave_re - band_re * wave_im
            for c in range(2):
                for m in range(len(ats)):
                    mates_out[m][c, :, cut] = mate_total[m][c].astype(mates_out[m].dtype)
                for g in range(groups):
                    for i in range(2):
                        sums[g][i, c, :, cut] = band_total[g][i][c].astype(sums[g].dtype)


def pair_terms(ats, flips, mates, bands, tables, sums=(), mate_sums=(), types=(jnp.bfloat16, jnp.float32)):
    groups = len(bands)
    jobs = len(ats) * groups
    vmem = pl.BlockSpec(memory_space=pltpu.VMEM)
    field = mates[0].shape
    operands = [*mates, *[band for group in bands for band in group], *sums, *mate_sums, *tables]
    out_shape = [jax.ShapeDtypeStruct(field, types[0])] * len(ats)
    out_shape += [jax.ShapeDtypeStruct((2,) + field, types[1])] * groups
    return pl.pallas_call(
        functools.partial(pair_kernel, ats, flips, len(sums) > 0, len(mate_sums) > 0),
        out_shape=out_shape,
        in_specs=[vmem] * len(operands),
        out_specs=[vmem] * len(out_shape),
        scratch_shapes=[
            pltpu.VMEM((2, jobs, 256, 256), jnp.bfloat16),
            pltpu.VMEM((8, jobs * 2 * GRID, 256), jnp.bfloat16),
            pltpu.VMEM((2, jobs, 256, 256), jnp.bfloat16),
        ],
        compiler_params=pltpu.CompilerParams(vmem_limit_bytes=VMEM_BYTES),
        cost_estimate=pl.CostEstimate(flops=jobs * 10**9, bytes_accessed=jobs * 10**6, transcendentals=0),
    )(*operands)


def passed_along(value, by):
    count = lax.axis_size("ka")
    return lax.ppermute(value, "ka", [(i, (i + by) % count) for i in range(count)])


def swapped(value, flip):
    return lax.ppermute(value, "ba", [(i, i ^ flip) for i in range(lax.axis_size("ba"))])


def on_device(orbitals, kpoints, occupied):
    own = orbitals[0, 0]
    spot = jnp.stack([lax.axis_index("ka"), lax.axis_index("ba")])
    tables = staged(kpoints.T, occupied, spot)
    near = (own, swapped(own, 2))
    far = (swapped(own, 1), swapped(near[1], 1))
    mates = [passed_along(own, step) for step in SHIFTS]
    near_flips, far_flips = (0, 2), (1, 3)
    *terms, near_sum, far_sum = pair_terms((0, 1, 2), (near_flips, far_flips), mates, (near, far), tables)
    from_core = swapped(far_sum.astype(jnp.bfloat16), 1)
    across = swapped((near_sum[1] + from_core[1].astype(jnp.float32)).astype(jnp.bfloat16), 2)
    back = [passed_along(term, -step) for term, step in zip(terms, SHIFTS)]
    total = near_sum[0] + from_core[0].astype(jnp.float32) + across.astype(jnp.float32)
    for returned in back:
        total = total + returned.astype(jnp.float32)
    return total[None, None]


def solution(mesh):
    in_specs = (P("ka", "ba", None, None, None), P(), P())
    out_specs = P("ka", "ba", None, None, None)
    return jax.shard_map(
        on_device, mesh=mesh, in_specs=in_specs, out_specs=out_specs, check_vma=False
    )
```

```python
import functools
import math

import jax
import jax.numpy as jnp
from jax import lax
from jax.experimental import pallas as pl
from jax.experimental.pallas import tpu as pltpu
from jax.sharding import PartitionSpec as P

KMESH = 8
SHIFTS = (-2, 1, 3)
GRID = 32
LANES = 128
CELL = 20.52
SCREENING = 0.05
VMEM_BYTES = 32 * 1024 * 1024


def block(index):
    return slice(index * LANES, (index + 1) * LANES)


def rows(index):
    return slice(index * GRID, (index + 1) * GRID)


def dot(left, right, dims=((1,), (0,))):
    return lax.dot_general(left, right, (dims, ((), ())), preferred_element_type=jnp.float32)


def stage_kernel(kpoints, occupied, spot, band, held, forward_x, inverse_x, forward_yz, inverse_yz, screened, weights):
    held[...] = band[...]
    turn = 2 * math.pi / GRID
    square = (LANES, LANES)
    row = lax.broadcasted_iota(jnp.int32, square, 0)
    column = lax.broadcasted_iota(jnp.int32, square, 1)
    row_high, column_high = lax.shift_right_logical(row, 5), lax.shift_right_logical(column, 5)

    def cosine_of(turns):
        turns = jnp.abs(jnp.bitwise_and(turns + GRID // 2, GRID - 1) - GRID // 2)
        folded = jnp.minimum(turns, GRID // 2 - turns).astype(jnp.float32)
        square = folded * folded * (turn * turn)
        series = 1.0
        for order in (10, 8, 6, 4, 2):
            series = 1.0 - square * series * (1.0 / (order * (order - 1)))
        return jnp.where(turns > GRID // 4, -series, series)

    def wave(turns):
        return cosine_of(turns), cosine_of(turns - GRID // 4)

    def put(table, at, upper, lower):
        table[at, :LANES] = jnp.concatenate(upper, axis=1).astype(table.dtype)
        table[at, LANES:] = jnp.concatenate(lower, axis=1).astype(table.dtype)

    low = jnp.bitwise_and(row, GRID - 1) * jnp.bitwise_and(column, GRID - 1)
    cosine, sine = wave(8 * row_high * column_high + low)
    row_cosine, row_sine = wave(row_high)
    column_cosine, column_sine = wave(column_high)
    down = across = (cosine, sine)
    for k1 in range(8):
        put(forward_yz, k1, (down[0], -down[1]), (down[1], down[0]))
        put(inverse_yz, k1, (across[0], across[1]), (-across[1], across[0]))
        if k1 % 4 == 0:
            put(forward_x, k1 // 4, (down[0], down[1]), (-down[1], down[0]))
            put(inverse_x, k1 // 4, (across[0], -across[1]), (across[1], across[0]))
        down = (
            down[0] * row_cosine - down[1] * row_sine,
            down[0] * row_sine + down[1] * row_cosine,
        )
        across = (
            across[0] * column_cosine - across[1] * column_sine,
            across[0] * column_sine + across[1] * column_cosine,
        )

    count = kpoints.shape[1]
    own = spot[0]
    slot = spot[1]
    unit = 2 * math.pi / CELL
    shape = (GRID, LANES)
    lane = lax.broadcasted_iota(jnp.int32, shape, 1)
    high = lax.shift_right_logical(lane, 5) * 8

    def centred(index):
        return (jnp.bitwise_and(index + GRID // 2, GRID - 1) - GRID // 2).astype(jnp.float32)

    def occupancy(point, band):
        return jnp.full((1, LANES), jnp.where(band < occupied[point], -1.0, 0.0), jnp.float32)

    grid_x = centred(lax.broadcasted_iota(jnp.int32, shape, 0))
    grid_z = centred(jnp.bitwise_and(lane, GRID - 1))
    for at, step in enumerate(SHIFTS):
        other = lax.rem(own - step + count, count)
        later, earlier = (own, other) if step > 0 else (other, own)
        along = []
        for i in range(3):
            apart = lax.rem(kpoints[i, later] - kpoints[i, earlier] + KMESH // 2 + KMESH, KMESH)
            along.append((apart - KMESH // 2).astype(jnp.float32) / KMESH)
        at_x = (grid_x + along[0]) * unit
        at_z = (grid_z + along[2]) * unit
        flat = at_x * at_x + at_z * at_z + SCREENING
        for k1 in range(8):
            at_y = (centred(high + k1) + along[1]) * unit
            screened[at, k1] = (math.pi / GRID**3) / (flat + at_y * at_y)
        weights[4 + at] = occupancy(other, slot)
    for flip in range(4):
        weights[flip] = occupancy(own, slot ^ flip)


def staged(kpoints, occupied, spot, band):
    smem = pl.BlockSpec(memory_space=pltpu.SMEM)
    vmem = pl.BlockSpec(memory_space=pltpu.VMEM)
    return pl.pallas_call(
        stage_kernel,
        out_shape=[
            jax.ShapeDtypeStruct(band.shape, band.dtype),
            jax.ShapeDtypeStruct((2, 256, 256), jnp.bfloat16),
            jax.ShapeDtypeStruct((2, 256, 256), jnp.bfloat16),
            jax.ShapeDtypeStruct((8, 256, 256), jnp.bfloat16),
            jax.ShapeDtypeStruct((8, 256, 256), jnp.bfloat16),
            jax.ShapeDtypeStruct((len(SHIFTS), 8, GRID, LANES), jnp.float32),
            jax.ShapeDtypeStruct((4 + len(SHIFTS), 1, LANES), jnp.float32),
        ],
        in_specs=[smem] * 3 + [vmem],
        out_specs=[vmem] * 7,
        compiler_params=pltpu.CompilerParams(vmem_limit_bytes=VMEM_BYTES),
        cost_estimate=pl.CostEstimate(flops=10**6, bytes_accessed=6 * 10**6, transcendentals=0),
    )(kpoints, occupied, spot, band)


def pair_kernel(ats, flips, has_sums, *refs):
    groups = len(flips)
    refs = list(refs)

    def take(n):
        taken = refs[:n]
        del refs[:n]
        return taken

    bands = [take(2) for _ in range(groups)]
    mates = take(len(ats))
    sums_in = take(groups) if has_sums else None
    forward_x, inverse_x, forward_yz, inverse_yz, screened, weights = take(6)
    mates_out = take(len(ats))
    sums = take(groups)
    wide, mid, back = refs
    jobs = [(m, g) for m in range(len(ats)) for g in range(groups)]

    for b in range(2):
        for a in range(4):
            cut = block(2 * a + b)
            for job, (m, g) in enumerate(jobs):
                mate_re = mates[m][0, :, cut].astype(jnp.float32)
                mate_im = mates[m][1, :, cut].astype(jnp.float32)
                for i in range(2):
                    band_re = bands[g][i][0, :, cut].astype(jnp.float32)
                    band_im = bands[g][i][1, :, cut].astype(jnp.float32)
                    value_re = mate_re * band_re + mate_im * band_im
                    if SHIFTS[ats[m]] < 0:
                        value_im = mate_im * band_re - mate_re * band_im
                    else:
                        value_im = mate_re * band_im - mate_im * band_re
                    wide[b, job, rows(a), block(i)] = value_re.astype(jnp.bfloat16)
                    wide[b, job, rows(4 + a), block(i)] = value_im.astype(jnp.bfloat16)

    for job in range(len(jobs)):
        even = dot(forward_x[0], wide[0, job])
        odd = dot(forward_x[1], wide[1, job])
        plus = (even + odd).astype(jnp.bfloat16)
        minus = (even - odd).astype(jnp.bfloat16)
        for i in range(2):
            for e in range(4):
                for c in range(2):
                    mid[e, rows(2 * job + i), block(c)] = plus[rows(4 * c + e), block(i)]
                    mid[e + 4, rows(2 * job + i), block(c)] = minus[rows(4 * c + e), block(i)]

    for e in range(4):
        halves = []
        for k1 in (e, e + 4):
            third = dot(mid[k1], forward_yz[k1])
            factor = []
            for at in ats:
                factor += [jnp.concatenate([screened[at, k1]] * 2, axis=1)] * (2 * groups)
            factor = jnp.concatenate(factor, axis=0)
            halves.append(dot((third * factor).astype(jnp.bfloat16), inverse_yz[k1]))
        for b in range(2):
            joined = (halves[0] - halves[1] if b else halves[0] + halves[1]).astype(jnp.bfloat16)
            for job in range(len(jobs)):
                for i in range(2):
                    for c in range(2):
                        back[b, job, rows(4 * c + e), block(i)] = joined[rows(2 * job + i), block(c)]

    for b in range(2):
        waves = [dot(inverse_x[b], back[b, job]) for job in range(len(jobs))]
        for a in range(4):
            cut = block(2 * a + b)
            mate_total = [[0.0, 0.0] for _ in ats]
            if has_sums:
                band_total = [[[s[i, c, :, cut] for c in range(2)] for i in range(2)] for s in sums_in]
            else:
                band_total = [[[0.0, 0.0] for _ in range(2)] for _ in flips]
            for job, (m, g) in enumerate(jobs):
                mate_weight = weights[4 + ats[m]]
                mate_re = mates[m][0, :, cut].astype(jnp.float32) * mate_weight
                mate_im = mates[m][1, :, cut].astype(jnp.float32) * mate_weight
                for i in range(2):
                    weight = weights[flips[g][i]]
                    wave_re = waves[job][rows(a), block(i)]
                    wave_im = waves[job][rows(4 + a), block(i)]
                    band_re = bands[g][i][0, :, cut].astype(jnp.float32) * weight
                    band_im = bands[g][i][1, :, cut].astype(jnp.float32) * weight
                    to_mate, to_band = mate_total[m], band_total[g][i]
                    if SHIFTS[ats[m]] < 0:
                        to_band[0] += mate_re * wave_re + mate_im * wave_im
                        to_band[1] += mate_im * wave_re - mate_re * wave_im
                        to_mate[0] += band_re * wave_re - band_im * wave_im
                        to_mate[1] += band_re * wave_im + band_im * wave_re
                    else:
                        to_band[0] += mate_re * wave_re - mate_im * wave_im
                        to_band[1] += mate_re * wave_im + mate_im * wave_re
                        to_mate[0] += band_re * wave_re + band_im * wave_im
                        to_mate[1] += band_im * wave_re - band_re * wave_im
            for c in range(2):
                for m in range(len(ats)):
                    mates_out[m][c, :, cut] = mate_total[m][c].astype(mates_out[m].dtype)
                for g in range(groups):
                    for i in range(2):
                        sums[g][i, c, :, cut] = band_total[g][i][c].astype(sums[g].dtype)


def pair_terms(ats, flips, mates, bands, tables, sums=(), types=(jnp.float32, jnp.float32)):
    groups = len(bands)
    jobs = len(ats) * groups
    vmem = pl.BlockSpec(memory_space=pltpu.VMEM)
    field = mates[0].shape
    operands = [*[band for group in bands for band in group], *mates, *sums, *tables]
    out_shape = [jax.ShapeDtypeStruct(field, jnp.bfloat16)] * len(ats)
    out_shape += [jax.ShapeDtypeStruct((2,) + field, kind) for kind in types]
    return pl.pallas_call(
        functools.partial(pair_kernel, ats, flips, len(sums) > 0),
        out_shape=out_shape,
        in_specs=[vmem] * len(operands),
        out_specs=[vmem] * len(out_shape),
        scratch_shapes=[
            pltpu.VMEM((2, jobs, 256, 256), jnp.bfloat16),
            pltpu.VMEM((8, jobs * 2 * GRID, 256), jnp.bfloat16),
            pltpu.VMEM((2, jobs, 256, 256), jnp.bfloat16),
        ],
        compiler_params=pltpu.CompilerParams(vmem_limit_bytes=VMEM_BYTES),
        cost_estimate=pl.CostEstimate(flops=jobs * 10**9, bytes_accessed=jobs * 10**6, transcendentals=0),
    )(*operands)


def passed_along(value, by):
    count = lax.axis_size("ka")
    return lax.ppermute(value, "ka", [(i, (i + by) % count) for i in range(count)])


def swapped(value, flip):
    return lax.ppermute(value, "ba", [(i, i ^ flip) for i in range(lax.axis_size("ba"))])


def on_device(orbitals, kpoints, occupied):
    own = orbitals[0, 0]
    spot = jnp.stack([lax.axis_index("ka"), lax.axis_index("ba")])
    held, *tables = staged(kpoints.T, occupied, spot, own)
    across = swapped(own, 2)
    near = (held, across)
    far = (swapped(own, 1), swapped(across, 1))
    mates = [passed_along(own, step) for step in SHIFTS]
    flips = ((0, 2), (1, 3))
    last = (jnp.float32, jnp.bfloat16)
    *terms, near_sum, far_sum = pair_terms((0, 1, 2), flips, mates, (near, far), tables, types=last)
    from_core = swapped(far_sum, 1)
    along = swapped((near_sum[1] + from_core[1].astype(jnp.float32)).astype(jnp.bfloat16), 2)
    back = [passed_along(terms[at], -SHIFTS[at]) for at in (0, 1, 2)]
    total = near_sum[0] + from_core[0].astype(jnp.float32) + along.astype(jnp.float32)
    for returned in back:
        total = total + returned.astype(jnp.float32)
    return total[None, None]


def solution(mesh):
    in_specs = (P("ka", "ba", None, None, None), P(), P())
    out_specs = P("ka", "ba", None, None, None)
    return jax.shard_map(
        on_device, mesh=mesh, in_specs=in_specs, out_specs=out_specs, check_vma=False
    )
```

```python
import functools
import math

import jax
import jax.numpy as jnp
from jax import lax
from jax.experimental import pallas as pl
from jax.experimental.pallas import tpu as pltpu
from jax.sharding import PartitionSpec as P

KMESH = 8
SHIFTS = ((2, 2, -3, -1), (3, 1, -1, -3), (-3, -1, 2, 2))
GRID = 32
LANES = 128
CELL = 20.52
SCREENING = 0.05
BANDS = 4
FLIPS = (0, 2, 1, 3)
VMEM_BYTES = 32 * 1024 * 1024


def block(index):
    return slice(index * LANES, (index + 1) * LANES)


def rows(index):
    return slice(index * GRID, (index + 1) * GRID)


def dot(left, right, dims=((1,), (0,))):
    return lax.dot_general(left, right, (dims, ((), ())), preferred_element_type=jnp.float32)


def table_kernel(forward_x, inverse_x, forward_yz, inverse_yz):
    turn = 2 * math.pi / GRID
    square = (LANES, LANES)
    row = lax.broadcasted_iota(jnp.int32, square, 0)
    column = lax.broadcasted_iota(jnp.int32, square, 1)
    row_high, column_high = lax.shift_right_logical(row, 5), lax.shift_right_logical(column, 5)

    def cosine_of(turns):
        turns = jnp.abs(jnp.bitwise_and(turns + GRID // 2, GRID - 1) - GRID // 2)
        folded = jnp.minimum(turns, GRID // 2 - turns).astype(jnp.float32)
        square = folded * folded * (turn * turn)
        series = 1.0
        for order in (10, 8, 6, 4, 2):
            series = 1.0 - square * series * (1.0 / (order * (order - 1)))
        return jnp.where(turns > GRID // 4, -series, series)

    def wave(turns):
        return cosine_of(turns), cosine_of(turns - GRID // 4)

    def put(table, at, upper, lower):
        table[at, :LANES] = jnp.concatenate(upper, axis=1).astype(table.dtype)
        table[at, LANES:] = jnp.concatenate(lower, axis=1).astype(table.dtype)

    low = jnp.bitwise_and(row, GRID - 1) * jnp.bitwise_and(column, GRID - 1)
    cosine, sine = wave(8 * row_high * column_high + low)
    row_cosine, row_sine = wave(row_high)
    column_cosine, column_sine = wave(column_high)
    down = across = (cosine, sine)
    for k1 in range(8):
        put(forward_yz, k1, (down[0], -down[1]), (down[1], down[0]))
        put(inverse_yz, k1, (across[0], across[1]), (-across[1], across[0]))
        if k1 % 4 == 0:
            put(forward_x, k1 // 4, (down[0], down[1]), (-down[1], down[0]))
            put(inverse_x, k1 // 4, (across[0], -across[1]), (across[1], across[0]))
        down = (
            down[0] * row_cosine - down[1] * row_sine,
            down[0] * row_sine + down[1] * row_cosine,
        )
        across = (
            across[0] * column_cosine - across[1] * column_sine,
            across[0] * column_sine + across[1] * column_cosine,
        )


def point_kernel(kpoints, occupied, spot, screened, weights):
    count = kpoints.shape[1]
    own = spot[0]
    slot = spot[1]
    unit = 2 * math.pi / CELL
    shape = (GRID, LANES)
    lane = lax.broadcasted_iota(jnp.int32, shape, 1)
    high = lax.shift_right_logical(lane, 5) * 8

    def centred(index):
        return (jnp.bitwise_and(index + GRID // 2, GRID - 1) - GRID // 2).astype(jnp.float32)

    def occupancy(point, band):
        return jnp.full((1, LANES), jnp.where(band < occupied[point], -1.0, 0.0), jnp.float32)

    grid_x = centred(lax.broadcasted_iota(jnp.int32, shape, 0))
    grid_z = centred(jnp.bitwise_and(lane, GRID - 1))
    for at, shifts in enumerate(SHIFTS):
        step = shifts[0]
        for turn in range(1, len(shifts)):
            step = jnp.where(lax.rem(own, len(shifts)) == turn, shifts[turn], step)
        other = lax.rem(own - step + count, count)
        later, earlier = jnp.where(step > 0, own, other), jnp.where(step > 0, other, own)
        along = []
        for i in range(3):
            apart = lax.rem(kpoints[i, later] - kpoints[i, earlier] + KMESH // 2 + KMESH, KMESH)
            along.append((apart - KMESH // 2).astype(jnp.float32) / KMESH)
        at_x = (grid_x + along[0]) * unit
        at_z = (grid_z + along[2]) * unit
        flat = at_x * at_x + at_z * at_z + SCREENING
        for k1 in range(8):
            at_y = (centred(high + k1) + along[1]) * unit
            screened[at, k1] = (math.pi / GRID**3) / (flat + at_y * at_y)
        weights[4 + at] = occupancy(other, slot)
        sign = jnp.where(step > 0, 1.0, -1.0)
        weights[7 + at] = jnp.full((1, LANES), sign, jnp.float32)
    for flip in range(4):
        weights[flip] = occupancy(own, slot ^ flip)


def tables_of(kpoints, occupied, spot):
    smem = pl.BlockSpec(memory_space=pltpu.SMEM)
    vmem = pl.BlockSpec(memory_space=pltpu.VMEM)
    params = pltpu.CompilerParams(vmem_limit_bytes=VMEM_BYTES)
    tables = pl.pallas_call(
        table_kernel,
        out_shape=[jax.ShapeDtypeStruct((count, 256, 256), jnp.bfloat16) for count in (2, 2, 8, 8)],
        out_specs=[vmem] * 4,
        compiler_params=params,
        cost_estimate=pl.CostEstimate(flops=2 * 10**9, bytes_accessed=3 * 10**6, transcendentals=0),
    )()
    points = pl.pallas_call(
        point_kernel,
        out_shape=[
            jax.ShapeDtypeStruct((len(SHIFTS), 8, GRID, LANES), jnp.float32),
            jax.ShapeDtypeStruct((4 + 2 * len(SHIFTS), 1, LANES), jnp.float32),
        ],
        in_specs=[smem] * 3,
        out_specs=[vmem] * 2,
        compiler_params=params,
        cost_estimate=pl.CostEstimate(flops=10**8, bytes_accessed=10**5, transcendentals=0),
    )(kpoints, occupied, spot)
    return (*tables, *points)


def pair_kernel(*refs):
    bands, mates = refs[:4], refs[4:7]
    forward_x, inverse_x, forward_yz, inverse_yz, screened, weights = refs[7:13]
    mates_out = refs[13:16]
    sums = [refs[16], refs[17], refs[18].at[0], refs[18].at[1]]
    wide, mid, back = refs[19:]
    signs = [weights[7 + m] for m in range(len(SHIFTS))]

    for b in range(2):
        for a in range(4):
            cut = block(2 * a + b)
            for n in range(BANDS):
                band_re = bands[n][0, :, cut].astype(jnp.float32)
                band_im = bands[n][1, :, cut].astype(jnp.float32)
                for m in range(len(SHIFTS)):
                    job, i = 2 * m + n // 2, n % 2
                    mate_re = mates[m][0, :, cut].astype(jnp.float32)
                    mate_im = mates[m][1, :, cut].astype(jnp.float32)
                    value_re = mate_re * band_re + mate_im * band_im
                    value_im = (mate_re * band_im - mate_im * band_re) * signs[m]
                    wide[b, job, rows(a), block(i)] = value_re.astype(jnp.bfloat16)
                    wide[b, job, rows(4 + a), block(i)] = value_im.astype(jnp.bfloat16)

    for job in range(2 * len(SHIFTS)):
        even = dot(forward_x[0], wide[0, job])
        odd = dot(forward_x[1], wide[1, job])
        plus = (even + odd).astype(jnp.bfloat16)
        minus = (even - odd).astype(jnp.bfloat16)
        for i in range(2):
            for e in range(4):
                for c in range(2):
                    mid[e, rows(2 * job + i), block(c)] = plus[rows(4 * c + e), block(i)]
                    mid[e + 4, rows(2 * job + i), block(c)] = minus[rows(4 * c + e), block(i)]

    for e in range(4):
        halves = []
        for k1 in (e, e + 4):
            third = dot(mid[k1], forward_yz[k1])
            factor = []
            for m in range(len(SHIFTS)):
                factor += [jnp.concatenate([screened[m, k1]] * 2, axis=1)] * BANDS
            factor = jnp.concatenate(factor, axis=0)
            halves.append(dot((third * factor).astype(jnp.bfloat16), inverse_yz[k1]))
        for b in range(2):
            joined = (halves[0] - halves[1] if b else halves[0] + halves[1]).astype(jnp.bfloat16)
            for job in range(2 * len(SHIFTS)):
                for i in range(2):
                    for c in range(2):
                        back[b, job, rows(4 * c + e), block(i)] = joined[rows(2 * job + i), block(c)]

    for b in range(2):
        waves = [dot(inverse_x[b], back[b, job]) for job in range(2 * len(SHIFTS))]
        for a in range(4):
            cut = block(2 * a + b)
            mate_total = [[0.0, 0.0] for _ in mates]
            band_total = [[0.0, 0.0] for _ in bands]
            for m in range(len(SHIFTS)):
                mate_re = mates[m][0, :, cut].astype(jnp.float32) * weights[4 + m]
                mate_im = mates[m][1, :, cut].astype(jnp.float32) * weights[4 + m]
                for n in range(BANDS):
                    band_re = bands[n][0, :, cut].astype(jnp.float32) * weights[FLIPS[n]]
                    band_im = bands[n][1, :, cut].astype(jnp.float32) * weights[FLIPS[n]]
                    wave_re = waves[2 * m + n // 2][rows(a), block(n % 2)]
                    wave_im = waves[2 * m + n // 2][rows(4 + a), block(n % 2)] * signs[m]
                    band_total[n][0] += mate_re * wave_re - mate_im * wave_im
                    band_total[n][1] += mate_re * wave_im + mate_im * wave_re
                    mate_total[m][0] += band_re * wave_re + band_im * wave_im
                    mate_total[m][1] += band_im * wave_re - band_re * wave_im
            for c in range(2):
                for m in range(len(SHIFTS)):
                    mates_out[m][c, :, cut] = mate_total[m][c].astype(mates_out[m].dtype)
                for n in range(BANDS):
                    sums[n][c, :, cut] = band_total[n][c].astype(sums[n].dtype)


def pair_terms(bands, mates, tables, short=jnp.bfloat16):
    vmem = pl.BlockSpec(memory_space=pltpu.VMEM)
    field = mates[0].shape
    jobs = 2 * len(SHIFTS)
    operands = [*bands, *mates, *tables]
    out_shape = [jax.ShapeDtypeStruct(field, kind) for kind in (short,) * len(SHIFTS) + (jnp.float32,) * 2]
    out_shape.append(jax.ShapeDtypeStruct((2,) + field, short))
    return pl.pallas_call(
        pair_kernel,
        out_shape=out_shape,
        in_specs=[vmem] * len(operands),
        out_specs=[vmem] * len(out_shape),
        scratch_shapes=[
            pltpu.VMEM((2, jobs, 256, 256), jnp.bfloat16),
            pltpu.VMEM((8, jobs * 2 * GRID, 256), jnp.bfloat16),
            pltpu.VMEM((2, jobs, 256, 256), jnp.bfloat16),
        ],
        compiler_params=pltpu.CompilerParams(vmem_limit_bytes=VMEM_BYTES),
        cost_estimate=pl.CostEstimate(flops=6 * 10**9, bytes_accessed=6 * 10**6, transcendentals=0),
    )(*operands)


def passed_along(value, shifts, back=False):
    count = lax.axis_size("ka")
    pairs = [((k - shifts[k % len(shifts)]) % count, k) for k in range(count)]
    if back:
        pairs = [(to, start) for start, to in pairs]
    return lax.ppermute(value, "ka", pairs)


def swapped(value, flip):
    return lax.ppermute(value, "ba", [(i, i ^ flip) for i in range(lax.axis_size("ba"))])


def on_device(orbitals, kpoints, occupied):
    own = orbitals[0, 0]
    spot = jnp.stack([lax.axis_index("ka"), lax.axis_index("ba")])
    tables = tables_of(kpoints.T, occupied, spot)
    across = swapped(own, 2)
    bands = (own, across, swapped(own, 1), swapped(across, 1))
    mates = [passed_along(own, shifts) for shifts in SHIFTS]
    *terms, own_sum, across_sum, far_sum = pair_terms(bands, mates, tables)
    beside, beyond = swapped(far_sum, 1)
    leaving = (across_sum + beyond.astype(jnp.float32)).astype(jnp.bfloat16)
    total = own_sum + beside.astype(jnp.float32) + swapped(leaving, 2).astype(jnp.float32)
    for at in (0, 1, 2):
        total = total + passed_along(terms[at], SHIFTS[at], back=True).astype(jnp.float32)
    return total[None, None]


def solution(mesh):
    in_specs = (P("ka", "ba", None, None, None), P(), P())
    out_specs = P("ka", "ba", None, None, None)
    return jax.shard_map(
        on_device, mesh=mesh, in_specs=in_specs, out_specs=out_specs, check_vma=False
    )
```

```python
import functools
import math

import jax
import jax.numpy as jnp
from jax import lax
from jax.experimental import pallas as pl
from jax.experimental.pallas import tpu as pltpu
from jax.sharding import PartitionSpec as P

KMESH = 8
SHIFTS = ((2, 2, -3, -1), (3, 1, -1, -3), (-3, -1, 2, 2))
GRID = 32
LANES = 128
CELL = 20.52
SCREENING = 0.05
BANDS = 4
FLIPS = (0, 2, 1, 3)
VMEM_BYTES = 32 * 1024 * 1024


def block(index):
    return slice(index * LANES, (index + 1) * LANES)


def rows(index):
    return slice(index * GRID, (index + 1) * GRID)


def dot(left, right, dims=((1,), (0,))):
    return lax.dot_general(left, right, (dims, ((), ())), preferred_element_type=jnp.float32)


def table_kernel(forward_x, inverse_x, forward_yz, inverse_yz):
    turn = 2 * math.pi / GRID
    square = (LANES, LANES)
    row = lax.broadcasted_iota(jnp.int32, square, 0)
    column = lax.broadcasted_iota(jnp.int32, square, 1)
    row_high, column_high = lax.shift_right_logical(row, 5), lax.shift_right_logical(column, 5)

    def cosine_of(turns):
        turns = jnp.abs(jnp.bitwise_and(turns + GRID // 2, GRID - 1) - GRID // 2)
        folded = jnp.minimum(turns, GRID // 2 - turns).astype(jnp.float32)
        square = folded * folded * (turn * turn)
        series = 1.0
        for order in (10, 8, 6, 4, 2):
            series = 1.0 - square * series * (1.0 / (order * (order - 1)))
        return jnp.where(turns > GRID // 4, -series, series)

    def wave(turns):
        return cosine_of(turns), cosine_of(turns - GRID // 4)

    def put(table, at, upper, lower):
        table[at, :LANES] = jnp.concatenate(upper, axis=1).astype(table.dtype)
        table[at, LANES:] = jnp.concatenate(lower, axis=1).astype(table.dtype)

    low = jnp.bitwise_and(row, GRID - 1) * jnp.bitwise_and(column, GRID - 1)
    cosine, sine = wave(8 * row_high * column_high + low)
    row_cosine, row_sine = wave(row_high)
    column_cosine, column_sine = wave(column_high)
    down = across = (cosine, sine)
    for k1 in range(8):
        put(forward_yz, k1, (down[0], -down[1]), (down[1], down[0]))
        put(inverse_yz, k1, (across[0], across[1]), (-across[1], across[0]))
        if k1 % 4 == 0:
            put(forward_x, k1 // 4, (down[0], down[1]), (-down[1], down[0]))
            put(inverse_x, k1 // 4, (across[0], -across[1]), (across[1], across[0]))
        down = (
            down[0] * row_cosine - down[1] * row_sine,
            down[0] * row_sine + down[1] * row_cosine,
        )
        across = (
            across[0] * column_cosine - across[1] * column_sine,
            across[0] * column_sine + across[1] * column_cosine,
        )


def point_kernel(kpoints, occupied, spot, screened, weights):
    count = kpoints.shape[1]
    own = spot[0]
    slot = spot[1]
    unit = 2 * math.pi / CELL
    shape = (GRID, LANES)
    lane = lax.broadcasted_iota(jnp.int32, shape, 1)
    high = lax.shift_right_logical(lane, 5) * 8

    def centred(index):
        return (jnp.bitwise_and(index + GRID // 2, GRID - 1) - GRID // 2).astype(jnp.float32)

    def occupancy(point, band):
        return jnp.full((1, LANES), jnp.where(band < occupied[point], -1.0, 0.0), jnp.float32)

    grid_x = centred(lax.broadcasted_iota(jnp.int32, shape, 0))
    grid_z = centred(jnp.bitwise_and(lane, GRID - 1))
    for at, shifts in enumerate(SHIFTS):
        step = shifts[0]
        for turn in range(1, len(shifts)):
            step = jnp.where(lax.rem(own, len(shifts)) == turn, shifts[turn], step)
        other = lax.rem(own - step + count, count)
        later, earlier = jnp.where(step > 0, own, other), jnp.where(step > 0, other, own)
        along = []
        for i in range(3):
            apart = lax.rem(kpoints[i, later] - kpoints[i, earlier] + KMESH // 2 + KMESH, KMESH)
            along.append((apart - KMESH // 2).astype(jnp.float32) / KMESH)
        at_x = (grid_x + along[0]) * unit
        at_z = (grid_z + along[2]) * unit
        flat = at_x * at_x + at_z * at_z + SCREENING
        for k1 in range(8):
            at_y = (centred(high + k1) + along[1]) * unit
            screened[at, k1] = (math.pi / GRID**3) / (flat + at_y * at_y)
        weights[4 + at] = occupancy(other, slot)
        sign = jnp.where(step > 0, 1.0, -1.0)
        weights[7 + at] = jnp.full((1, LANES), sign, jnp.float32)
    for flip in range(4):
        weights[flip] = occupancy(own, slot ^ flip)


def tables_of(kpoints, occupied, spot):
    smem = pl.BlockSpec(memory_space=pltpu.SMEM)
    vmem = pl.BlockSpec(memory_space=pltpu.VMEM)
    params = pltpu.CompilerParams(vmem_limit_bytes=VMEM_BYTES)
    tables = pl.pallas_call(
        table_kernel,
        out_shape=[jax.ShapeDtypeStruct((count, 256, 256), jnp.bfloat16) for count in (2, 2, 8, 8)],
        out_specs=[vmem] * 4,
        compiler_params=params,
        cost_estimate=pl.CostEstimate(flops=2 * 10**9, bytes_accessed=3 * 10**6, transcendentals=0),
    )()
    points = pl.pallas_call(
        point_kernel,
        out_shape=[
            jax.ShapeDtypeStruct((len(SHIFTS), 8, GRID, LANES), jnp.float32),
            jax.ShapeDtypeStruct((4 + 2 * len(SHIFTS), 1, LANES), jnp.float32),
        ],
        in_specs=[smem] * 3,
        out_specs=[vmem] * 2,
        compiler_params=params,
        cost_estimate=pl.CostEstimate(flops=10**8, bytes_accessed=10**5, transcendentals=0),
    )(kpoints, occupied, spot)
    return (*tables, *points)


def pair_kernel(*refs):
    bands, mates = refs[:4], refs[4:7]
    forward_x, inverse_x, forward_yz, inverse_yz, screened, weights = refs[7:13]
    mates_out = refs[13:16]
    sums = [refs[16], refs[17], refs[18].at[0], refs[18].at[1]]
    wide, mid, back = refs[19:]
    signs = [weights[7 + m] for m in range(len(SHIFTS))]

    for b in range(2):
        for a in range(4):
            cut = block(2 * a + b)
            for n in range(BANDS):
                band_re = bands[n][0, :, cut].astype(jnp.float32)
                band_im = bands[n][1, :, cut].astype(jnp.float32)
                for m in range(len(SHIFTS)):
                    job, i = 2 * m + n // 2, n % 2
                    mate_re = mates[m][0, :, cut].astype(jnp.float32)
                    mate_im = mates[m][1, :, cut].astype(jnp.float32)
                    value_re = mate_re * band_re + mate_im * band_im
                    value_im = (mate_re * band_im - mate_im * band_re) * signs[m]
                    wide[b, job, rows(a), block(i)] = value_re.astype(jnp.bfloat16)
                    wide[b, job, rows(4 + a), block(i)] = value_im.astype(jnp.bfloat16)

    for job in range(2 * len(SHIFTS)):
        even = dot(forward_x[0], wide[0, job])
        odd = dot(forward_x[1], wide[1, job])
        plus = (even + odd).astype(jnp.bfloat16)
        minus = (even - odd).astype(jnp.bfloat16)
        for i in range(2):
            for e in range(4):
                for c in range(2):
                    mid[e, rows(2 * job + i), block(c)] = plus[rows(4 * c + e), block(i)]
                    mid[e + 4, rows(2 * job + i), block(c)] = minus[rows(4 * c + e), block(i)]

    for e in range(4):
        halves = []
        for k1 in (e, e + 4):
            third = dot(mid[k1], forward_yz[k1])
            factor = []
            for m in range(len(SHIFTS)):
                factor += [jnp.concatenate([screened[m, k1]] * 2, axis=1)] * BANDS
            factor = jnp.concatenate(factor, axis=0)
            halves.append(dot((third * factor).astype(jnp.bfloat16), inverse_yz[k1]))
        for b in range(2):
            joined = (halves[0] - halves[1] if b else halves[0] + halves[1]).astype(jnp.bfloat16)
            for job in range(2 * len(SHIFTS)):
                for i in range(2):
                    for c in range(2):
                        back[b, job, rows(4 * c + e), block(i)] = joined[rows(2 * job + i), block(c)]

    for b in range(2):
        waves = [dot(inverse_x[b], back[b, job]) for job in range(2 * len(SHIFTS))]
        for a in range(4):
            cut = block(2 * a + b)
            mate_total = [[0.0, 0.0] for _ in mates]
            band_total = [[0.0, 0.0] for _ in bands]
            for m in range(len(SHIFTS)):
                mate_re = mates[m][0, :, cut].astype(jnp.float32) * weights[4 + m]
                mate_im = mates[m][1, :, cut].astype(jnp.float32) * weights[4 + m]
                for n in range(BANDS):
                    band_re = bands[n][0, :, cut].astype(jnp.float32) * weights[FLIPS[n]]
                    band_im = bands[n][1, :, cut].astype(jnp.float32) * weights[FLIPS[n]]
                    wave_re = waves[2 * m + n // 2][rows(a), block(n % 2)]
                    wave_im = waves[2 * m + n // 2][rows(4 + a), block(n % 2)] * signs[m]
                    band_total[n][0] += mate_re * wave_re - mate_im * wave_im
                    band_total[n][1] += mate_re * wave_im + mate_im * wave_re
                    mate_total[m][0] += band_re * wave_re + band_im * wave_im
                    mate_total[m][1] += band_im * wave_re - band_re * wave_im
            for c in range(2):
                for m in range(len(SHIFTS)):
                    mates_out[m][c, :, cut] = mate_total[m][c].astype(mates_out[m].dtype)
                for n in range(BANDS):
                    sums[n][c, :, cut] = band_total[n][c].astype(sums[n].dtype)


def pair_terms(bands, mates, tables, short=jnp.bfloat16):
    vmem = pl.BlockSpec(memory_space=pltpu.VMEM)
    field = mates[0].shape
    jobs = 2 * len(SHIFTS)
    operands = [*bands, *mates, *tables]
    out_shape = [jax.ShapeDtypeStruct(field, kind) for kind in (short,) * len(SHIFTS) + (jnp.float32,) * 2]
    out_shape.append(jax.ShapeDtypeStruct((2,) + field, short))
    return pl.pallas_call(
        pair_kernel,
        out_shape=out_shape,
        in_specs=[vmem] * len(operands),
        out_specs=[vmem] * len(out_shape),
        scratch_shapes=[
            pltpu.VMEM((2, jobs, 256, 256), jnp.bfloat16),
            pltpu.VMEM((8, jobs * 2 * GRID, 256), jnp.bfloat16),
            pltpu.VMEM((2, jobs, 256, 256), jnp.bfloat16),
        ],
        compiler_params=pltpu.CompilerParams(vmem_limit_bytes=VMEM_BYTES),
        cost_estimate=pl.CostEstimate(flops=6 * 10**9, bytes_accessed=6 * 10**6, transcendentals=0),
    )(*operands)


def passed_along(value, shifts, back=False):
    count = lax.axis_size("ka")
    pairs = [((k - shifts[k % len(shifts)]) % count, k) for k in range(count)]
    if back:
        pairs = [(to, start) for start, to in pairs]
    return lax.ppermute(value, "ka", pairs)


def swapped(value, flip):
    return lax.ppermute(value, "ba", [(i, i ^ flip) for i in range(lax.axis_size("ba"))])


def on_device(orbitals, kpoints, occupied):
    own = orbitals[0, 0]
    spot = jnp.stack([lax.axis_index("ka"), lax.axis_index("ba")])
    tables = tables_of(kpoints.T, occupied, spot)
    across = swapped(own, 2)
    bands = (own, across, swapped(own, 1), swapped(across, 1))
    mates = [passed_along(own, shifts) for shifts in SHIFTS]
    *terms, own_sum, across_sum, far_sum = pair_terms(bands, mates, tables)
    beside, beyond = swapped(far_sum, 1)
    leaving = (across_sum + beyond.astype(jnp.float32)).astype(jnp.bfloat16)
    total = own_sum + beside.astype(jnp.float32) + swapped(leaving, 2).astype(jnp.float32)
    for at in (0, 2, 1):
        total = total + passed_along(terms[at], SHIFTS[at], back=True).astype(jnp.float32)
    return total[None, None]


def solution(mesh):
    in_specs = (P("ka", "ba", None, None, None), P(), P())
    out_specs = P("ka", "ba", None, None, None)
    return jax.shard_map(
        on_device, mesh=mesh, in_specs=in_specs, out_specs=out_specs, check_vma=False
    )
```

```python
import functools
import math

import jax
import jax.numpy as jnp
from jax import lax
from jax.experimental import pallas as pl
from jax.experimental.pallas import tpu as pltpu
from jax.sharding import PartitionSpec as P

KMESH = 8
SHIFTS = ((2, 2, -3, -1), (3, 1, -1, -3), (-3, -1, 2, 2))
GRID = 32
LANES = 128
CELL = 20.52
SCREENING = 0.05
BANDS = 4
FLIPS = (0, 2, 1, 3)
VMEM_BYTES = 32 * 1024 * 1024


def block(index):
    return slice(index * LANES, (index + 1) * LANES)


def rows(index):
    return slice(index * GRID, (index + 1) * GRID)


def dot(left, right, dims=((1,), (0,))):
    return lax.dot_general(left, right, (dims, ((), ())), preferred_element_type=jnp.float32)


def table_kernel(forward_x, inverse_x, forward_yz, inverse_yz):
    turn = 2 * math.pi / GRID
    square = (LANES, LANES)
    row = lax.broadcasted_iota(jnp.int32, square, 0)
    column = lax.broadcasted_iota(jnp.int32, square, 1)
    row_high, column_high = lax.shift_right_logical(row, 5), lax.shift_right_logical(column, 5)

    def cosine_of(turns):
        turns = jnp.abs(jnp.bitwise_and(turns + GRID // 2, GRID - 1) - GRID // 2)
        folded = jnp.minimum(turns, GRID // 2 - turns).astype(jnp.float32)
        square = folded * folded * (turn * turn)
        series = 1.0
        for order in (10, 8, 6, 4, 2):
            series = 1.0 - square * series * (1.0 / (order * (order - 1)))
        return jnp.where(turns > GRID // 4, -series, series)

    def wave(turns):
        return cosine_of(turns), cosine_of(turns - GRID // 4)

    def put(table, at, upper, lower):
        table[at, :LANES] = jnp.concatenate(upper, axis=1).astype(table.dtype)
        table[at, LANES:] = jnp.concatenate(lower, axis=1).astype(table.dtype)

    low = jnp.bitwise_and(row, GRID - 1) * jnp.bitwise_and(column, GRID - 1)
    cosine, sine = wave(8 * row_high * column_high + low)
    row_cosine, row_sine = wave(row_high)
    column_cosine, column_sine = wave(column_high)
    down = across = (cosine, sine)
    for k1 in range(8):
        put(forward_yz, k1, (down[0], -down[1]), (down[1], down[0]))
        put(inverse_yz, k1, (across[0], across[1]), (-across[1], across[0]))
        if k1 % 4 == 0:
            put(forward_x, k1 // 4, (down[0], down[1]), (-down[1], down[0]))
            put(inverse_x, k1 // 4, (across[0], -across[1]), (across[1], across[0]))
        down = (
            down[0] * row_cosine - down[1] * row_sine,
            down[0] * row_sine + down[1] * row_cosine,
        )
        across = (
            across[0] * column_cosine - across[1] * column_sine,
            across[0] * column_sine + across[1] * column_cosine,
        )


def point_kernel(kpoints, occupied, spot, screened, weights):
    count = kpoints.shape[1]
    own = spot[0]
    slot = spot[1]
    unit = 2 * math.pi / CELL
    shape = (GRID, LANES)
    lane = lax.broadcasted_iota(jnp.int32, shape, 1)
    high = lax.shift_right_logical(lane, 5) * 8

    def centred(index):
        return (jnp.bitwise_and(index + GRID // 2, GRID - 1) - GRID // 2).astype(jnp.float32)

    def occupancy(point, band):
        return jnp.full((1, LANES), jnp.where(band < occupied[point], -1.0, 0.0), jnp.float32)

    grid_x = centred(lax.broadcasted_iota(jnp.int32, shape, 0))
    grid_z = centred(jnp.bitwise_and(lane, GRID - 1))
    for at, shifts in enumerate(SHIFTS):
        step = shifts[0]
        for turn in range(1, len(shifts)):
            step = jnp.where(lax.rem(own, len(shifts)) == turn, shifts[turn], step)
        other = lax.rem(own - step + count, count)
        later, earlier = jnp.where(step > 0, own, other), jnp.where(step > 0, other, own)
        along = []
        for i in range(3):
            apart = lax.rem(kpoints[i, later] - kpoints[i, earlier] + KMESH // 2 + KMESH, KMESH)
            along.append((apart - KMESH // 2).astype(jnp.float32) / KMESH)
        at_x = (grid_x + along[0]) * unit
        at_z = (grid_z + along[2]) * unit
        flat = at_x * at_x + at_z * at_z + SCREENING
        for k1 in range(8):
            at_y = (centred(high + k1) + along[1]) * unit
            screened[at, k1] = (math.pi / GRID**3) / (flat + at_y * at_y)
        weights[4 + at] = occupancy(other, slot)
        sign = jnp.where(step > 0, 1.0, -1.0)
        weights[7 + at] = jnp.full((1, LANES), sign, jnp.float32)
    for flip in range(4):
        weights[flip] = occupancy(own, slot ^ flip)


def tables_of(kpoints, occupied, spot):
    smem = pl.BlockSpec(memory_space=pltpu.SMEM)
    vmem = pl.BlockSpec(memory_space=pltpu.VMEM)
    params = pltpu.CompilerParams(vmem_limit_bytes=VMEM_BYTES)
    tables = pl.pallas_call(
        table_kernel,
        out_shape=[jax.ShapeDtypeStruct((count, 256, 256), jnp.bfloat16) for count in (2, 2, 8, 8)],
        out_specs=[vmem] * 4,
        compiler_params=params,
        cost_estimate=pl.CostEstimate(flops=2 * 10**9, bytes_accessed=3 * 10**6, transcendentals=0),
    )()
    points = pl.pallas_call(
        point_kernel,
        out_shape=[
            jax.ShapeDtypeStruct((len(SHIFTS), 8, GRID, LANES), jnp.float32),
            jax.ShapeDtypeStruct((4 + 2 * len(SHIFTS), 1, LANES), jnp.float32),
        ],
        in_specs=[smem] * 3,
        out_specs=[vmem] * 2,
        compiler_params=params,
        cost_estimate=pl.CostEstimate(flops=10**8, bytes_accessed=10**5, transcendentals=0),
    )(kpoints, occupied, spot)
    return (*tables, *points)


def pair_kernel(*refs):
    bands, mates = refs[:4], refs[4:7]
    forward_x, inverse_x, forward_yz, inverse_yz, screened, weights = refs[7:13]
    mates_out = refs[13:16]
    sums = [refs[16], refs[17], refs[18].at[0], refs[18].at[1]]
    wide, mid, back = refs[19:]
    signs = [weights[7 + m] for m in range(len(SHIFTS))]

    for b in range(2):
        for a in range(4):
            cut = block(2 * a + b)
            for n in range(BANDS):
                band_re = bands[n][0, :, cut].astype(jnp.float32)
                band_im = bands[n][1, :, cut].astype(jnp.float32)
                for m in range(len(SHIFTS)):
                    job, i = 2 * m + n // 2, n % 2
                    mate_re = mates[m][0, :, cut].astype(jnp.float32)
                    mate_im = mates[m][1, :, cut].astype(jnp.float32)
                    value_re = mate_re * band_re + mate_im * band_im
                    value_im = (mate_re * band_im - mate_im * band_re) * signs[m]
                    wide[b, job, rows(a), block(i)] = value_re.astype(jnp.bfloat16)
                    wide[b, job, rows(4 + a), block(i)] = value_im.astype(jnp.bfloat16)

    for job in range(2 * len(SHIFTS)):
        even = dot(forward_x[0], wide[0, job])
        odd = dot(forward_x[1], wide[1, job])
        plus = (even + odd).astype(jnp.bfloat16)
        minus = (even - odd).astype(jnp.bfloat16)
        for i in range(2):
            for e in range(4):
                for c in range(2):
                    mid[e, rows(2 * job + i), block(c)] = plus[rows(4 * c + e), block(i)]
                    mid[e + 4, rows(2 * job + i), block(c)] = minus[rows(4 * c + e), block(i)]

    for k1 in range(8):
        factor = []
        for m in range(len(SHIFTS)):
            factor += [jnp.concatenate([screened[m, k1]] * 2, axis=1)] * BANDS
        factor = jnp.concatenate(factor, axis=0)
        mid[k1] = (dot(mid[k1], forward_yz[k1]) * factor).astype(jnp.bfloat16)
    for e in range(4):
        halves = [dot(mid[k1], inverse_yz[k1]) for k1 in (e, e + 4)]
        for b in range(2):
            joined = (halves[0] - halves[1] if b else halves[0] + halves[1]).astype(jnp.bfloat16)
            for job in range(2 * len(SHIFTS)):
                for i in range(2):
                    for c in range(2):
                        back[b, job, rows(4 * c + e), block(i)] = joined[rows(2 * job + i), block(c)]

    for b in range(2):
        waves = [dot(inverse_x[b], back[b, job]) for job in range(2 * len(SHIFTS))]
        for a in range(4):
            cut = block(2 * a + b)
            mate_total = [[0.0, 0.0] for _ in mates]
            band_total = [[0.0, 0.0] for _ in bands]
            for m in range(len(SHIFTS)):
                mate_re = mates[m][0, :, cut].astype(jnp.float32) * weights[4 + m]
                mate_im = mates[m][1, :, cut].astype(jnp.float32) * weights[4 + m]
                for n in range(BANDS):
                    band_re = bands[n][0, :, cut].astype(jnp.float32) * weights[FLIPS[n]]
                    band_im = bands[n][1, :, cut].astype(jnp.float32) * weights[FLIPS[n]]
                    wave_re = waves[2 * m + n // 2][rows(a), block(n % 2)]
                    wave_im = waves[2 * m + n // 2][rows(4 + a), block(n % 2)] * signs[m]
                    band_total[n][0] += mate_re * wave_re - mate_im * wave_im
                    band_total[n][1] += mate_re * wave_im + mate_im * wave_re
                    mate_total[m][0] += band_re * wave_re + band_im * wave_im
                    mate_total[m][1] += band_im * wave_re - band_re * wave_im
            for c in range(2):
                for m in range(len(SHIFTS)):
                    mates_out[m][c, :, cut] = mate_total[m][c].astype(mates_out[m].dtype)
                for n in range(BANDS):
                    sums[n][c, :, cut] = band_total[n][c].astype(sums[n].dtype)


def pair_terms(bands, mates, tables, short=jnp.bfloat16):
    vmem = pl.BlockSpec(memory_space=pltpu.VMEM)
    field = mates[0].shape
    jobs = 2 * len(SHIFTS)
    operands = [*bands, *mates, *tables]
    out_shape = [jax.ShapeDtypeStruct(field, kind) for kind in (short,) * len(SHIFTS) + (jnp.float32,) * 2]
    out_shape.append(jax.ShapeDtypeStruct((2,) + field, short))
    return pl.pallas_call(
        pair_kernel,
        out_shape=out_shape,
        in_specs=[vmem] * len(operands),
        out_specs=[vmem] * len(out_shape),
        scratch_shapes=[
            pltpu.VMEM((2, jobs, 256, 256), jnp.bfloat16),
            pltpu.VMEM((8, jobs * 2 * GRID, 256), jnp.bfloat16),
            pltpu.VMEM((2, jobs, 256, 256), jnp.bfloat16),
        ],
        compiler_params=pltpu.CompilerParams(vmem_limit_bytes=VMEM_BYTES),
        cost_estimate=pl.CostEstimate(flops=6 * 10**9, bytes_accessed=6 * 10**6, transcendentals=0),
    )(*operands)


def passed_along(value, shifts, back=False):
    count = lax.axis_size("ka")
    pairs = [((k - shifts[k % len(shifts)]) % count, k) for k in range(count)]
    if back:
        pairs = [(to, start) for start, to in pairs]
    return lax.ppermute(value, "ka", pairs)


def swapped(value, flip):
    return lax.ppermute(value, "ba", [(i, i ^ flip) for i in range(lax.axis_size("ba"))])


def on_device(orbitals, kpoints, occupied):
    own = orbitals[0, 0]
    spot = jnp.stack([lax.axis_index("ka"), lax.axis_index("ba")])
    tables = tables_of(kpoints.T, occupied, spot)
    across = swapped(own, 2)
    bands = (own, across, swapped(own, 1), swapped(across, 1))
    mates = [passed_along(own, shifts) for shifts in SHIFTS]
    *terms, own_sum, across_sum, far_sum = pair_terms(bands, mates, tables)
    beside, beyond = swapped(far_sum, 1)
    leaving = (across_sum + beyond.astype(jnp.float32)).astype(jnp.bfloat16)
    total = own_sum + beside.astype(jnp.float32) + swapped(leaving, 2).astype(jnp.float32)
    for at in (0, 2, 1):
        total = total + passed_along(terms[at], SHIFTS[at], back=True).astype(jnp.float32)
    return total[None, None]


def solution(mesh):
    in_specs = (P("ka", "ba", None, None, None), P(), P())
    out_specs = P("ka", "ba", None, None, None)
    return jax.shard_map(
        on_device, mesh=mesh, in_specs=in_specs, out_specs=out_specs, check_vma=False
    )
```

```python
import functools
import math

import jax
import jax.numpy as jnp
from jax import lax
from jax.experimental import pallas as pl
from jax.experimental.pallas import tpu as pltpu
from jax.sharding import PartitionSpec as P

KMESH = 8
SHIFTS = ((2, 2, -3, -1), (3, 1, -1, -3), (-3, -1, 2, 2))
GRID = 32
LANES = 128
CELL = 20.52
SCREENING = 0.05
BANDS = 4
FLIPS = (0, 2, 1, 3)
VMEM_BYTES = 32 * 1024 * 1024


def block(index):
    return slice(index * LANES, (index + 1) * LANES)


def rows(index):
    return slice(index * GRID, (index + 1) * GRID)


def dot(left, right, dims=((1,), (0,))):
    return lax.dot_general(left, right, (dims, ((), ())), preferred_element_type=jnp.float32)


def table_kernel(forward_x, inverse_x, forward_yz, inverse_yz):
    turn = 2 * math.pi / GRID
    square = (LANES, LANES)
    row = lax.broadcasted_iota(jnp.int32, square, 0)
    column = lax.broadcasted_iota(jnp.int32, square, 1)
    row_high, column_high = lax.shift_right_logical(row, 5), lax.shift_right_logical(column, 5)

    def cosine_of(turns):
        turns = jnp.abs(jnp.bitwise_and(turns + GRID // 2, GRID - 1) - GRID // 2)
        folded = jnp.minimum(turns, GRID // 2 - turns).astype(jnp.float32)
        square = folded * folded * (turn * turn)
        series = 1.0
        for order in (10, 8, 6, 4, 2):
            series = 1.0 - square * series * (1.0 / (order * (order - 1)))
        return jnp.where(turns > GRID // 4, -series, series)

    def wave(turns):
        return cosine_of(turns), cosine_of(turns - GRID // 4)

    def put(table, at, upper, lower):
        table[at, :LANES] = jnp.concatenate(upper, axis=1).astype(table.dtype)
        table[at, LANES:] = jnp.concatenate(lower, axis=1).astype(table.dtype)

    low = jnp.bitwise_and(row, GRID - 1) * jnp.bitwise_and(column, GRID - 1)
    cosine, sine = wave(8 * row_high * column_high + low)
    row_cosine, row_sine = wave(row_high)
    column_cosine, column_sine = wave(column_high)
    down = across = (cosine, sine)
    for k1 in range(8):
        put(forward_yz, k1, (down[0], -down[1]), (down[1], down[0]))
        put(inverse_yz, k1, (across[0], across[1]), (-across[1], across[0]))
        if k1 % 4 == 0:
            put(forward_x, k1 // 4, (down[0], down[1]), (-down[1], down[0]))
            put(inverse_x, k1 // 4, (across[0], -across[1]), (across[1], across[0]))
        down = (
            down[0] * row_cosine - down[1] * row_sine,
            down[0] * row_sine + down[1] * row_cosine,
        )
        across = (
            across[0] * column_cosine - across[1] * column_sine,
            across[0] * column_sine + across[1] * column_cosine,
        )


def point_kernel(kpoints, occupied, spot, screened, weights):
    count = kpoints.shape[1]
    own = spot[0]
    slot = spot[1]
    unit = 2 * math.pi / CELL
    shape = (GRID, LANES)
    lane = lax.broadcasted_iota(jnp.int32, shape, 1)
    high = lax.shift_right_logical(lane, 5) * 8

    def centred(index):
        return (jnp.bitwise_and(index + GRID // 2, GRID - 1) - GRID // 2).astype(jnp.float32)

    def occupancy(point, band):
        return jnp.full((1, LANES), jnp.where(band < occupied[point], -1.0, 0.0), jnp.float32)

    grid_x = centred(lax.broadcasted_iota(jnp.int32, shape, 0))
    grid_z = centred(jnp.bitwise_and(lane, GRID - 1))
    for at, shifts in enumerate(SHIFTS):
        step = shifts[0]
        for turn in range(1, len(shifts)):
            step = jnp.where(lax.rem(own, len(shifts)) == turn, shifts[turn], step)
        other = lax.rem(own - step + count, count)
        later, earlier = jnp.where(step > 0, own, other), jnp.where(step > 0, other, own)
        along = []
        for i in range(3):
            apart = lax.rem(kpoints[i, later] - kpoints[i, earlier] + KMESH // 2 + KMESH, KMESH)
            along.append((apart - KMESH // 2).astype(jnp.float32) / KMESH)
        at_x = (grid_x + along[0]) * unit
        at_z = (grid_z + along[2]) * unit
        flat = at_x * at_x + at_z * at_z + SCREENING
        for k1 in range(8):
            at_y = (centred(high + k1) + along[1]) * unit
            screened[at, k1] = (math.pi / GRID**3) / (flat + at_y * at_y)
        weights[4 + at] = occupancy(other, slot)
        sign = jnp.where(step > 0, 1.0, -1.0)
        weights[7 + at] = jnp.full((1, LANES), sign, jnp.float32)
    for flip in range(4):
        weights[flip] = occupancy(own, slot ^ flip)


def tables_of(kpoints, occupied, spot):
    smem = pl.BlockSpec(memory_space=pltpu.SMEM)
    vmem = pl.BlockSpec(memory_space=pltpu.VMEM)
    params = pltpu.CompilerParams(vmem_limit_bytes=VMEM_BYTES)
    tables = pl.pallas_call(
        table_kernel,
        out_shape=[jax.ShapeDtypeStruct((count, 256, 256), jnp.bfloat16) for count in (2, 2, 8, 8)],
        out_specs=[vmem] * 4,
        compiler_params=params,
        cost_estimate=pl.CostEstimate(flops=10**8, bytes_accessed=10**5, transcendentals=0),
    )()
    points = pl.pallas_call(
        point_kernel,
        out_shape=[
            jax.ShapeDtypeStruct((len(SHIFTS), 8, GRID, LANES), jnp.float32),
            jax.ShapeDtypeStruct((4 + 2 * len(SHIFTS), 1, LANES), jnp.float32),
        ],
        in_specs=[smem] * 3,
        out_specs=[vmem] * 2,
        compiler_params=params,
        cost_estimate=pl.CostEstimate(flops=2 * 10**9, bytes_accessed=10**5, transcendentals=0),
    )(kpoints, occupied, spot)
    return (*tables, *points)


def pair_kernel(*refs):
    bands, mates = refs[:4], refs[4:7]
    forward_x, inverse_x, forward_yz, inverse_yz, screened, weights = refs[7:13]
    mates_out = refs[13:16]
    sums = [refs[16], refs[17], refs[18].at[0], refs[18].at[1]]
    wide, mid, back = refs[19:]
    signs = [weights[7 + m] for m in range(len(SHIFTS))]
    short_signs = [sign.astype(jnp.bfloat16) for sign in signs]

    for b in range(2):
        for a in range(4):
            cut = block(2 * a + b)
            for n in range(BANDS):
                band_re, band_im = bands[n][0, :, cut], bands[n][1, :, cut]
                for m in range(len(SHIFTS)):
                    job, i = 2 * m + n // 2, n % 2
                    mate_re, mate_im = mates[m][0, :, cut], mates[m][1, :, cut]
                    value_im = mate_re * band_im - mate_im * band_re
                    wide[b, job, rows(a), block(i)] = mate_re * band_re + mate_im * band_im
                    wide[b, job, rows(4 + a), block(i)] = value_im * short_signs[m]

    for job in range(2 * len(SHIFTS)):
        even = dot(forward_x[0], wide[0, job])
        odd = dot(forward_x[1], wide[1, job])
        plus = (even + odd).astype(jnp.bfloat16)
        minus = (even - odd).astype(jnp.bfloat16)
        for i in range(2):
            for e in range(4):
                for c in range(2):
                    mid[e, rows(2 * job + i), block(c)] = plus[rows(4 * c + e), block(i)]
                    mid[e + 4, rows(2 * job + i), block(c)] = minus[rows(4 * c + e), block(i)]

    for k1 in range(8):
        factor = []
        for m in range(len(SHIFTS)):
            factor += [jnp.concatenate([screened[m, k1]] * 2, axis=1)] * BANDS
        factor = jnp.concatenate(factor, axis=0)
        mid[k1] = (dot(mid[k1], forward_yz[k1]) * factor).astype(jnp.bfloat16)
    for e in range(4):
        halves = [dot(mid[k1], inverse_yz[k1]) for k1 in (e, e + 4)]
        for b in range(2):
            joined = (halves[0] - halves[1] if b else halves[0] + halves[1]).astype(jnp.bfloat16)
            for job in range(2 * len(SHIFTS)):
                for i in range(2):
                    for c in range(2):
                        back[b, job, rows(4 * c + e), block(i)] = joined[rows(2 * job + i), block(c)]

    for b in range(2):
        waves = [dot(inverse_x[b], back[b, job]) for job in range(2 * len(SHIFTS))]
        for a in range(4):
            cut = block(2 * a + b)
            mate_total = [[0.0, 0.0] for _ in mates]
            band_total = [[0.0, 0.0] for _ in bands]
            for m in range(len(SHIFTS)):
                mate_re = mates[m][0, :, cut].astype(jnp.float32) * weights[4 + m]
                mate_im = mates[m][1, :, cut].astype(jnp.float32) * weights[4 + m]
                for n in range(BANDS):
                    band_re = bands[n][0, :, cut].astype(jnp.float32) * weights[FLIPS[n]]
                    band_im = bands[n][1, :, cut].astype(jnp.float32) * weights[FLIPS[n]]
                    wave_re = waves[2 * m + n // 2][rows(a), block(n % 2)]
                    wave_im = waves[2 * m + n // 2][rows(4 + a), block(n % 2)] * signs[m]
                    band_total[n][0] += mate_re * wave_re - mate_im * wave_im
                    band_total[n][1] += mate_re * wave_im + mate_im * wave_re
                    mate_total[m][0] += band_re * wave_re + band_im * wave_im
                    mate_total[m][1] += band_im * wave_re - band_re * wave_im
            for c in range(2):
                for m in range(len(SHIFTS)):
                    mates_out[m][c, :, cut] = mate_total[m][c].astype(mates_out[m].dtype)
                for n in range(BANDS):
                    sums[n][c, :, cut] = band_total[n][c].astype(sums[n].dtype)


def pair_terms(bands, mates, tables, short=jnp.bfloat16):
    vmem = pl.BlockSpec(memory_space=pltpu.VMEM)
    field = mates[0].shape
    jobs = 2 * len(SHIFTS)
    operands = [*bands, *mates, *tables]
    out_shape = [jax.ShapeDtypeStruct(field, kind) for kind in (short,) * len(SHIFTS) + (jnp.float32,) * 2]
    out_shape.append(jax.ShapeDtypeStruct((2,) + field, short))
    return pl.pallas_call(
        pair_kernel,
        out_shape=out_shape,
        in_specs=[vmem] * len(operands),
        out_specs=[vmem] * len(out_shape),
        scratch_shapes=[
            pltpu.VMEM((2, jobs, 256, 256), jnp.bfloat16),
            pltpu.VMEM((8, jobs * 2 * GRID, 256), jnp.bfloat16),
            pltpu.VMEM((2, jobs, 256, 256), jnp.bfloat16),
        ],
        compiler_params=pltpu.CompilerParams(vmem_limit_bytes=VMEM_BYTES),
        cost_estimate=pl.CostEstimate(flops=6 * 10**9, bytes_accessed=6 * 10**6, transcendentals=0),
    )(*operands)


def passed_along(value, shifts, back=False):
    count = lax.axis_size("ka")
    pairs = [((k - shifts[k % len(shifts)]) % count, k) for k in range(count)]
    if back:
        pairs = [(to, start) for start, to in pairs]
    return lax.ppermute(value, "ka", pairs)


def swapped(value, flip):
    return lax.ppermute(value, "ba", [(i, i ^ flip) for i in range(lax.axis_size("ba"))])


def on_device(orbitals, kpoints, occupied):
    own = orbitals[0, 0]
    spot = jnp.stack([lax.axis_index("ka"), lax.axis_index("ba")])
    tables = tables_of(kpoints.T, occupied, spot)
    across = swapped(own, 2)
    bands = (own, across, swapped(own, 1), swapped(across, 1))
    mates = [passed_along(own, shifts) for shifts in SHIFTS]
    *terms, own_sum, across_sum, far_sum = pair_terms(bands, mates, tables)
    beside, beyond = swapped(far_sum, 1)
    leaving = (across_sum + beyond.astype(jnp.float32)).astype(jnp.bfloat16)
    total = own_sum + beside.astype(jnp.float32) + swapped(leaving, 2).astype(jnp.float32)
    for at in (0, 2, 1):
        total = total + passed_along(terms[at], SHIFTS[at], back=True).astype(jnp.float32)
    return total[None, None]


def solution(mesh):
    in_specs = (P("ka", "ba", None, None, None), P(), P())
    out_specs = P("ka", "ba", None, None, None)
    return jax.shard_map(
        on_device, mesh=mesh, in_specs=in_specs, out_specs=out_specs, check_vma=False
    )
```
